32 devices in a mesh: row: 16 (over z, y, core), col: 2 (over x).
Axes of the slice: x: 2, y: 2, z: 4, core: 2. Of those that a mesh axis runs over, the one named last changes fastest.
Arguments:
- features: bfloat16 [128, 4096], P(None, ('row', 'col')), may hold values from -6 to 6
- positions: float32 [3, 4096], P(None, ('row', 'col')), may hold values from 0 to 6
- tile_pairs: int32 [16, 2, 2, 4], P('row', 'col'), may hold values from 0 to 15, as said below
- pair_count: int32 [16, 2], P('row', 'col'), may hold values from 1 to 4, as said below
- masks: int32 [16, 2, 4, 128, 128], P('row', 'col'), may hold values 0 or 1
- w_in: bfloat16 [128, 128], replicated, may hold values from -0.5 to 0.5
- w_f1: bfloat16 [64, 128], replicated, may hold values from -3 to 3
- b_f1: float32 [128], replicated, may hold values from -3 to 3
- w_f2: bfloat16 [128, 128], replicated, may hold values from -0.1875 to 0.1875
- b_f2: float32 [128], replicated, may hold values from -2 to 2
- w_o1: bfloat16 [128, 128], replicated, may hold values from -0.25 to 0.25
- b_o1: float32 [128], replicated, may hold values from -3 to 3
- w_o2: bfloat16 [128, 128], replicated, may hold values from -0.5 to 0.5
- b_o2: float32 [128], replicated, may hold values from -3 to 3
- read_w: float32 [128], replicated, may hold values from -2 to 2
Outputs:
- features_out: bfloat16 [128, 4096], P(None, ('row', 'col'))
- forces: float32 [3, 4096], P(None, ('row', 'col'))
The draws below stay inside these ranges and needn't reach their ends.
Inputs may be any that keep to these rules, and one draw needn't show every extreme that they name: Only slots 0 to pair_count[r, c] - 1 of tile_pairs and masks of block (r, c) are listed. tile_pairs[r, c, 0, s] is a receiver tile below 2, tile_pairs[r, c, 1, s] a sender tile below 16; the slots of one grid block hold distinct tile pairs.
All inputs are finite; a program needn't handle non-finite values. No bound on the sum of `masks` on one device may be relied on, other than what follows from the above.
Results may differ from the reference program's by a relative error of at most 0.0075.
Values may be sent and summed in bfloat16 or wider, within the bound.
No kernel may reach another device: no remote copies, remote signals or barrier semaphores. Data moves between devices by JAX's collectives and lax.ppermute only.
A program may use at most 64 MiB of HBM per device.

```python
import math
import jax
import jax.numpy as jnp
from jax import lax

F = 128
NB = 64
FH = 128
TILE = 128
TP_MAX = 4
ATOM_DEV = 128
ATOMS = 4096
ROW_BLOCK = 256
N_ROW = 16
N_COL = 2


def draw_pair_count(key, part):
    key_light, key_busy, key_chosen = jax.random.split(key, 3)
    device_total = N_ROW * N_COL
    light_counts = jax.random.randint(key_light, (device_total,), 1, TP_MAX // 2 + 1)
    busy_draw = jax.random.randint(key_busy, (device_total,), 0, 8)
    counts = jnp.where(busy_draw == 0, TP_MAX, light_counts)
    chosen = jax.random.randint(key_chosen, (), 0, device_total)
    counts = counts.at[chosen].set(TP_MAX)
    return counts.reshape(N_ROW, N_COL).astype(jnp.int32)


def draw_tile_pairs(key, part):
    row_tiles = N_COL * ATOM_DEV // TILE
    col_tiles = N_ROW * ATOM_DEV // TILE
    device_keys = jax.random.split(key, N_ROW * N_COL)

    def choose(one_key):
        return jax.random.permutation(one_key, row_tiles * col_tiles)[:TP_MAX]
    picks = jax.vmap(choose)(device_keys)
    stacked = jnp.stack([picks // col_tiles, picks % col_tiles], axis=1)
    return stacked.reshape(N_ROW, N_COL, 2, TP_MAX).astype(jnp.int32)


def set_ends(entries, rng, low, top_value):
    longest = entries.shape.index(max(entries.shape))
    spots = []
    for shift in (0, 1):
        where = [jax.random.randint(jax.random.fold_in(rng, axis), (), 0, length) for axis, length in enumerate(entries.shape)]
        where[longest] = (where[longest] + shift) % entries.shape[longest]
        spots.append(tuple(where))
    return entries.at[spots[0]].set(low).at[spots[1]].set(top_value)


def levels(own_key, shape, pieces, smallest, largest):
    level, own = 1.0, jax.random.fold_in(own_key, 6)
    for axis_at, blocks in pieces:
        steps = jnp.exp(jax.random.uniform(jax.random.fold_in(own, axis_at), (blocks,), jnp.float32, smallest / len(pieces), largest / len(pieces)))
        level = level * jnp.repeat(steps, shape[axis_at] // blocks).reshape([-1 if axis == axis_at else 1 for axis in range(len(shape))])
    return level


def scatter_about(own_key, shape, deviation, reach, cuts=(), kind=jnp.bfloat16):
    drawn = jax.random.normal(own_key, shape, jnp.float32) * deviation
    if len(cuts) > 0:
        drawn = levels(own_key, shape, cuts, -0.22, 0.18) * drawn
    return jnp.clip(drawn, min=-reach, max=reach).astype(kind)


def setup_inputs(seed: int = 0) -> dict:
    keys = jax.random.split(jax.random.key(seed), 16)
    features = scatter_about(keys[0], (F, ATOMS), 1.0, 6.0, ((1, 32),))
    positions = jnp.clip(6.0 * jax.random.uniform(keys[1], (3, ATOMS), jnp.float32) ** levels(keys[1], (3, ATOMS), ((1, 32),), -0.2, 0.2), 0.0, 6.0)
    tile_pairs = draw_tile_pairs(jax.random.fold_in(keys[15], 71), 0)
    pair_count = draw_pair_count(jax.random.fold_in(keys[15], 71), 0)
    masks = set_ends((jax.random.randint(keys[4], (N_ROW, N_COL, TP_MAX, TILE, TILE), 0, 4) < 3).astype(jnp.int32), jax.random.fold_in(keys[4], 1), 0, 1)
    w_in = scatter_about(keys[5], (F, F), F ** -0.5, 0.5)
    w_f1 = scatter_about(keys[6], (NB, FH), 4 ** -0.5, 3.0)
    b_f1 = scatter_about(keys[7], (FH,), 0.5, 3.0, (), jnp.float32)
    w_f2 = scatter_about(keys[8], (FH, F), (8 * FH) ** -0.5, 0.1875)
    b_f2 = scatter_about(keys[9], (F,), 0.3, 2.0, (), jnp.float32)
    w_o1 = scatter_about(keys[10], (F, F), (4 * F) ** -0.5, 0.25)
    b_o1 = scatter_about(keys[11], (F,), 0.5, 3.0, (), jnp.float32)
    w_o2 = scatter_about(keys[12], (F, F), F ** -0.5, 0.5)
    b_o2 = scatter_about(keys[13], (F,), 0.5, 3.0, (), jnp.float32)
    read_w = scatter_about(keys[14], (F,), 0.3, 2.0, (), jnp.float32)
    return {"features": features, "positions": positions, "tile_pairs": tile_pairs, "pair_count": pair_count, "masks": masks, "w_in": w_in, "w_f1": w_f1, "b_f1": b_f1, "w_f2": w_f2, "b_f2": b_f2, "w_o1": w_o1, "b_o1": b_o1, "w_o2": w_o2, "b_o2": b_o2, "read_w": read_w}


SOFTENING = 0.25
GAMMA_RBF = 10.0
CENTER_MAX = 10.0
CUTOFF = 12.0

def shifted_softplus(value):
    return jax.nn.softplus(value) - math.log(2.0)

def einsum_wide(form, left, right):
    return jnp.einsum(form, left.astype(jnp.float32), right.astype(jnp.float32))

def filter_forward(distance, w_f1, b_f1, w_f2, b_f2):
    nbasis = w_f1.shape[0]
    centers = (jnp.arange(nbasis, dtype=jnp.float32) * (CENTER_MAX / (nbasis - 1)))[:, None, None]
    offset = distance[None] - centers
    gauss = jnp.exp(-GAMMA_RBF * offset * offset)
    basis = gauss.astype(jnp.bfloat16)
    hidden_pre = einsum_wide('kh,krc->hrc', w_f1, basis) + b_f1[:, None, None]
    hidden = shifted_softplus(hidden_pre).astype(jnp.bfloat16)
    filter_base = einsum_wide('hf,hrc->frc', w_f2, hidden) + b_f2[:, None, None]
    cutoff = 0.5 * (jnp.cos(math.pi / CUTOFF * distance) + 1.0)
    return (offset, gauss, hidden_pre, filter_base, cutoff)

def pair_geometry(pos_rows, pos_cols):
    separation = pos_rows[:, :, None] - pos_cols[:, None, :]
    distance = jnp.sqrt(lax.optimization_barrier(jnp.sum(separation * separation, axis=0)) + SOFTENING)
    return (separation, distance)

def block_messages(pos_rows, pos_cols, sender_feats, pair_mask, params):
    separation, distance = pair_geometry(pos_rows, pos_cols)
    offset, gauss, hidden_pre, filter_base, cutoff = filter_forward(distance, *params)
    weighted = filter_base * (cutoff * pair_mask)[None]
    return lax.optimization_barrier(jnp.sum(weighted * sender_feats.astype(jnp.float32)[:, None, :], axis=2))

def block_forces(pos_rows, pos_cols, sender_feats, grad_rows, pair_mask, params):
    w_f1, b_f1, w_f2, b_f2 = params
    separation, distance = pair_geometry(pos_rows, pos_cols)
    offset, gauss, hidden_pre, filter_base, cutoff = filter_forward(distance, *params)
    pair_grad = grad_rows[:, :, None] * sender_feats.astype(jnp.float32)[:, None, :] * pair_mask[None]
    filter_grad = (pair_grad * cutoff[None]).astype(jnp.bfloat16)
    cutoff_grad = lax.optimization_barrier(jnp.sum(pair_grad * filter_base, axis=0))
    hidden_grad = einsum_wide('hf,frc->hrc', w_f2, filter_grad)
    hidden_grad = (hidden_grad * jax.nn.sigmoid(hidden_pre)).astype(jnp.bfloat16)
    basis_grad = einsum_wide('kh,hrc->krc', w_f1, hidden_grad)
    dist_grad = -2.0 * GAMMA_RBF * lax.optimization_barrier(jnp.sum(basis_grad * gauss * offset, axis=0))
    dist_grad = dist_grad - 0.5 * math.pi / CUTOFF * jnp.sin(math.pi / CUTOFF * distance) * cutoff_grad
    push = separation * (dist_grad / distance)[None]
    return (-lax.optimization_barrier(jnp.sum(push, axis=2)), lax.optimization_barrier(jnp.sum(push, axis=1)))

def tile_messages(pos_rows, pos_cols, sender_feats, pair_mask, params):
    rows = pos_rows.shape[1]
    block_rows = min(8, rows)
    block_count = rows // block_rows

    def per_block(block_index):
        start = block_index * block_rows
        return block_messages(lax.dynamic_slice_in_dim(pos_rows, start, block_rows, 1), pos_cols, sender_feats, lax.dynamic_slice_in_dim(pair_mask, start, block_rows, 0), params)
    parts = lax.map(per_block, jnp.arange(block_count, dtype=jnp.int32))
    return jnp.transpose(parts, (1, 0, 2)).reshape(parts.shape[1], rows)

def tile_forces(pos_rows, pos_cols, sender_feats, grad_rows, pair_mask, params):
    rows = pos_rows.shape[1]
    block_rows = min(8, rows)
    block_count = rows // block_rows

    def per_block(block_index):
        start = block_index * block_rows
        return block_forces(lax.dynamic_slice_in_dim(pos_rows, start, block_rows, 1), pos_cols, sender_feats, lax.dynamic_slice_in_dim(grad_rows, start, block_rows, 1), lax.dynamic_slice_in_dim(pair_mask, start, block_rows, 0), params)
    row_parts, col_parts = lax.map(per_block, jnp.arange(block_count, dtype=jnp.int32))
    return (jnp.transpose(row_parts, (1, 0, 2)).reshape(3, rows), lax.optimization_barrier(jnp.sum(col_parts, axis=0)))

def reference(features, positions, tile_pairs, pair_count, masks, w_in, w_f1, b_f1, w_f2, b_f2, w_o1, b_o1, w_o2, b_o2, read_w):
    params = (w_f1, b_f1, w_f2, b_f2)
    projected = einsum_wide('fo,fa->oa', w_in, features).astype(jnp.bfloat16)

    def locate(device_index, slot_index):
        row_index = device_index // N_COL
        col_index = device_index % N_COL
        row_tile = tile_pairs[row_index, col_index, 0, slot_index]
        col_tile = tile_pairs[row_index, col_index, 1, slot_index]
        row_start = row_index * ROW_BLOCK + row_tile * TILE
        local = col_tile * TILE
        col_start = (local // ATOM_DEV * N_COL + col_index) * ATOM_DEV + local % ATOM_DEV
        pair_mask = masks[row_index, col_index, slot_index].astype(jnp.float32)
        return (row_start.astype(jnp.int32), col_start.astype(jnp.int32), pair_mask)

    def count_of(device_index):
        return pair_count[device_index // N_COL, device_index % N_COL]

    def forward_device(totals, device_index):

        def per_slot(slot_index, inner):
            row_start, col_start, pair_mask = locate(device_index, slot_index)
            pos_rows = lax.dynamic_slice_in_dim(positions, row_start, TILE, 1)
            pos_cols = lax.dynamic_slice_in_dim(positions, col_start, TILE, 1)
            sender_feats = lax.dynamic_slice_in_dim(projected, col_start, TILE, 1)
            tile_sum = tile_messages(pos_rows, pos_cols, sender_feats, pair_mask, params)
            current = lax.dynamic_slice_in_dim(inner, row_start, TILE, 1)
            return lax.dynamic_update_slice_in_dim(inner, current + tile_sum, row_start, 1)
        return (lax.fori_loop(jnp.int32(0), count_of(device_index), per_slot, totals), None)
    device_ids = jnp.arange(N_ROW * N_COL, dtype=jnp.int32)
    messages, _ = lax.scan(forward_device, jnp.zeros((F, ATOMS), jnp.float32), device_ids)
    pre_act = einsum_wide('fo,fa->oa', w_o1, messages.astype(jnp.bfloat16)) + b_o1[:, None]
    activated = shifted_softplus(pre_act).astype(jnp.bfloat16)
    update = einsum_wide('fo,fa->oa', w_o2, activated) + b_o2[:, None]
    features_out = (features.astype(jnp.float32) + update).astype(jnp.bfloat16)
    direction = jnp.dot(w_o2.astype(jnp.float32), read_w, precision=lax.Precision.HIGHEST)
    message_grad = jnp.dot(w_o1.astype(jnp.float32), direction[:, None] * jax.nn.sigmoid(pre_act), precision=lax.Precision.HIGHEST)

    def backward_device(totals, device_index):

        def per_slot(slot_index, inner):
            row_start, col_start, pair_mask = locate(device_index, slot_index)
            pos_rows = lax.dynamic_slice_in_dim(positions, row_start, TILE, 1)
            pos_cols = lax.dynamic_slice_in_dim(positions, col_start, TILE, 1)
            sender_feats = lax.dynamic_slice_in_dim(projected, col_start, TILE, 1)
            grad_rows = lax.dynamic_slice_in_dim(message_grad, row_start, TILE, 1)
            row_part, col_part = tile_forces(pos_rows, pos_cols, sender_feats, grad_rows, pair_mask, params)
            current = lax.dynamic_slice_in_dim(inner, row_start, TILE, 1)
            inner = lax.dynamic_update_slice_in_dim(inner, current + row_part, row_start, 1)
            current = lax.dynamic_slice_in_dim(inner, col_start, TILE, 1)
            return lax.dynamic_update_slice_in_dim(inner, current + col_part, col_start, 1)
        return (lax.fori_loop(jnp.int32(0), count_of(device_index), per_slot, totals), None)
    forces, _ = lax.scan(backward_device, jnp.zeros((3, ATOMS), jnp.float32), device_ids)
    return (features_out, forces)
```

```python
import functools
import math

import jax
import jax.numpy as jnp
from jax import lax
from jax.experimental import pallas as pl
from jax.experimental.pallas import tpu as pltpu
from jax.sharding import PartitionSpec as P

SOFTENING = 0.25
GAMMA_RBF = 10.0
CENTER_MAX = 10.0
CUTOFF = 12.0
LOG2E = math.log2(math.e)
SCALE = math.sqrt(GAMMA_RBF * LOG2E)
TANGENT = -GAMMA_RBF / (SCALE * LOG2E)
POS_ROWS = 16
CHUNK = 16
F32 = jnp.float32
BF16 = jnp.bfloat16


def dot(a, b):
    return jnp.dot(a, b, preferred_element_type=F32)


def dot_t(a, b):
    return lax.dot_general(a, b, (((1,), (1,)), ((), ())), preferred_element_type=F32)


def split2(x):
    hi = x.astype(BF16)
    return hi, (x - hi.astype(F32)).astype(BF16)


def fold(x):
    half = x.shape[0] // 2
    return jnp.concatenate([x[:half], x[half:]], axis=1)


def unfold(x):
    half = x.shape[1] // 2
    return jnp.concatenate([x[:, :half], x[:, half:]], axis=0)


def block_diag(x):
    zero = jnp.zeros_like(x)
    return jnp.concatenate(
        [jnp.concatenate([x, zero], axis=1), jnp.concatenate([zero, x], axis=1)], axis=0
    )


def reverse_bits(value, count):
    bits = count.bit_length() - 1
    out = jnp.int32(0)
    for k in range(bits):
        out = out | (((value >> k) & 1) << (bits - 1 - k))
    return out


def pair_kernel(
    n_row, info, near, far, col_pos, masks, w_in, w_f1, b_f1, w_f2, b_f2,
    msg, tangents, proj_out, geom_out,
    lhs, w2, w_in_t, diag, dist, coef_h, coef_x, coef_t, rows,
):
    slot, chunk = pl.program_id(0), pl.program_id(1)
    nbasis = w_f1.shape[0]
    hidden = w_f1.shape[1]
    tile = masks.shape[-1]
    tp = masks.shape[0]

    @pl.when((slot == 0) & (chunk == 0))
    def _():
        weights = w_f1[...].astype(F32)
        zero = jnp.zeros_like(weights)
        bias = b_f1[...] * LOG2E - 1.0
        b_hi = bias.astype(BF16).astype(F32)
        b_mid = (bias - b_hi).astype(BF16).astype(F32)
        b_lo = bias - b_hi - b_mid
        extra = jnp.concatenate([b_hi, b_mid, b_lo, jnp.zeros((13, hidden), F32)], axis=0)
        table = jnp.concatenate(
            [
                jnp.concatenate([weights, zero], axis=1),
                jnp.concatenate([zero, weights], axis=1),
                jnp.concatenate([extra, jnp.zeros_like(extra)], axis=1),
                jnp.zeros((256 - 2 * nbasis - 16, 2 * hidden), F32),
            ],
            axis=0,
        )
        lhs[...] = table.T[:, : 2 * nbasis + 16].astype(BF16)
        wide = w_f2[...].astype(F32)
        w2[...] = jnp.concatenate([wide, wide], axis=1)
        w_in_t[...] = w_in[...].astype(F32).T.astype(BF16)
        msg[...] = jnp.zeros_like(msg)

    @pl.when(slot < info[2])
    def _():
        @pl.when(chunk == 0)
        def _():
            row_tile, col_tile = info[3 + slot], info[3 + tp + slot]
            place = reverse_bits(col_tile ^ info[0], n_row)
            half = n_row // 2
            index = place & (half - 1)
            block = jnp.where(place >= half, far[index], near[index])
            proj = dot(w_in_t[...], block[:tile]).astype(BF16)
            proj_out[0] = proj
            proj_t = proj.astype(F32).T.astype(BF16)
            diag[...] = block_diag(proj_t)
            pieces = block[tile:].astype(F32)
            sender = pieces[0:3] + pieces[3:6] + pieces[6:9]
            receiver = col_pos[row_tile ^ info[1]]
            square = jnp.zeros((tile, tile), F32)
            separation = []
            for k in range(3):
                up = jnp.broadcast_to(receiver[k : k + 1], (tile, tile)).T
                separation.append(up - sender[k : k + 1])
                square = square + separation[k] * separation[k]
            distance = jnp.sqrt(square + SOFTENING)
            angle = (math.pi / CUTOFF) * distance
            mask = masks[slot].astype(F32)
            cut = 0.5 * (jnp.cos(angle) + 1.0) * mask
            slope = (-0.5 * math.pi / CUTOFF) * jnp.sin(angle) * mask
            dist[...] = fold(distance * SCALE)
            coef_h[...] = fold(cut)
            coef_x[...] = fold(slope)
            coef_t[...] = fold(cut * TANGENT)
            inverse = 1.0 / distance
            for k in range(3):
                geom_out[0, k] = fold(separation[k] * inverse)
            geom_out[0, 3] = fold(slope)
            c_hi, c_lo = split2(cut)
            bias_part = (dot(c_hi, proj_t) + dot(c_lo, proj_t)) * b_f2[...]
            here = pl.ds(pl.multiple_of(row_tile * tile, tile), tile)
            msg[here, :] = msg[here, :] + bias_part

        centers = lax.broadcasted_iota(jnp.int32, (nbasis, 2 * tile), 0).astype(F32) * (
            SCALE * CENTER_MAX / (nbasis - 1)
        )
        shift = math.log2(LOG2E)
        ones = jnp.ones((16, 2 * tile), BF16)

        @pl.loop(0, CHUNK // 8)
        def _(group):
            base = pl.multiple_of(chunk * CHUNK + group * 8, 8)
            d8 = dist[pl.ds(base, 8), :]
            h8 = coef_h[pl.ds(base, 8), :]
            x8 = coef_x[pl.ds(base, 8), :]
            t8 = coef_t[pl.ds(base, 8), :]
            sums = []
            for u in range(8):
                offset = d8[u : u + 1] - centers
                gauss = jnp.exp2(shift - offset * offset)
                basis = jnp.concatenate(
                    [gauss.astype(BF16), (offset * gauss).astype(BF16), ones], axis=0
                )
                pre = dot(lhs[...], basis)
                total = 0.5 + jnp.exp2(pre[:hidden])
                value = jnp.log(total)
                slope = (2.0 - pl.reciprocal(total, approx=True)) * pre[hidden:]
                left = (h8[u : u + 1] * value).astype(BF16)
                tangents[0, group * 8 + u] = (
                    x8[u : u + 1] * value + t8[u : u + 1] * slope
                ).astype(BF16)
                mixed = dot(left, diag[...])
                sums.append(jnp.sum(mixed * w2[...], axis=0, keepdims=True))
            rows[pl.ds(base, 8), :] = jnp.concatenate(sums, axis=0)

        @pl.when(chunk == pl.num_programs(1) - 1)
        def _():
            here = pl.ds(pl.multiple_of(info[3 + slot] * tile, tile), tile)
            msg[here, :] = msg[here, :] + unfold(rows[...])


def force_kernel(
    n_row, tp, info, msg_a, msg_b, features, w_o1, b_o1, w_o2, b_o2, read_w, w_f2, b_f2, proj, geom, tangents,
    features_out, col_force, row_force,
    w2, grads, pre_act, diag, grad_rows, rows,
):
    slot, chunk = pl.program_id(0), pl.program_id(1)
    tile = features.shape[1]

    @pl.when((slot == 0) & (chunk == 0))
    def _():
        col_force[...] = jnp.zeros_like(col_force)
        row_force[...] = jnp.zeros_like(row_force)
        wide = w_f2[...].astype(F32)
        w2[...] = jnp.concatenate([wide, wide], axis=1)
        messages = (msg_a[...] + msg_b[...]).astype(BF16)
        pre = dot(messages, w_o1[...]) + b_o1[...]
        pre_act[...] = pre
        own = pre_act[pl.ds(pl.multiple_of(info[1] * tile, tile), tile), :]
        active = jnp.maximum(own, 0.0) + jnp.log(1.0 + jnp.exp(-jnp.abs(own))) - math.log(2.0)
        update = dot(active.astype(BF16), w_o2[...]) + b_o2[...]
        features_out[...] = (features[...].astype(F32) + update.T).astype(BF16)
        readout = jnp.broadcast_to(read_w[...], (8, tile))
        r_hi = readout.astype(BF16)
        rest = readout - r_hi.astype(F32)
        r_mid, r_lo = split2(rest)
        direction = (
            dot_t(r_hi, w_o2[...]) + (dot_t(r_mid, w_o2[...]) + dot_t(r_lo, w_o2[...]))
        )[0:1]
        s_hi, s_lo = split2(direction / (1.0 + jnp.exp(-pre)))
        grads[...] = dot_t(s_hi, w_o1[...]) + dot_t(s_lo, w_o1[...])

    @pl.when(slot < info[2])
    def _():
        @pl.when(chunk == 0)
        def _():
            here = pl.ds(pl.multiple_of(info[3 + slot] * tile, tile), tile)
            grad_rows[...] = fold(grads[here, :])
            diag[...] = block_diag(proj[0])

        @pl.loop(0, CHUNK // 8)
        def _(group):
            base = pl.multiple_of(chunk * CHUNK + group * 8, 8)
            g8 = grad_rows[pl.ds(base, 8), :]
            sums = []
            for u in range(8):
                left = (w2[...] * g8[u : u + 1]).astype(BF16)
                mixed = dot(left, diag[...])
                sums.append(
                    jnp.sum(mixed * tangents[0, group * 8 + u].astype(F32), axis=0, keepdims=True)
                )
            rows[pl.ds(base, 8), :] = jnp.concatenate(sums, axis=0)

        @pl.when(chunk == pl.num_programs(1) - 1)
        def _():
            row_tile, col_tile = info[3 + slot], info[3 + tp + slot]
            g_hi, g_lo = split2(unfold(grad_rows[...]) * b_f2[...])
            bias_part = dot(g_hi, proj[0]) + dot(g_lo, proj[0])
            dist_grad = unfold(rows[...]) + unfold(geom[0, 3]) * bias_part
            to_rows, to_cols = [], []
            for k in range(3):
                push = unfold(geom[0, k]) * dist_grad
                to_cols.append(jnp.sum(push, axis=0, keepdims=True))
                to_rows.append(-jnp.sum(push.T, axis=0, keepdims=True))
            zero = jnp.zeros((5, tile), F32)
            place = reverse_bits(col_tile ^ info[0], n_row)
            col_force[place] = col_force[place] + jnp.concatenate(to_cols + [zero], axis=0)
            n_col = row_force.shape[0]
            place = reverse_bits(row_tile ^ info[1], n_col)
            row_force[place] = row_force[place] + jnp.concatenate(to_rows + [zero], axis=0)


def exchange(value, axis, size, step):
    return lax.ppermute(value, axis, [(i, i ^ step) for i in range(size)])


def whole(shape):
    return pl.BlockSpec(shape, lambda s, c, info: (0,) * len(shape))


def local(
    features, positions, tile_pairs, pair_count, masks,
    w_in, w_f1, b_f1, w_f2, b_f2, w_o1, b_o1, w_o2, b_o2, read_w,
):
    n_feat, owned = features.shape
    tile = masks.shape[-1]
    tp = masks.shape[2]
    n_row = lax.axis_size("row")
    n_col = lax.axis_size("col")
    row_index = lax.axis_index("row")
    col_index = lax.axis_index("col")
    span = n_col * owned
    half = tile // 2
    chunks = half // CHUNK

    p_hi = lax.reduce_precision(positions, 8, 7)
    p_mid = lax.reduce_precision(positions - p_hi, 8, 7)
    p_lo = positions - p_hi - p_mid
    pieces = jnp.concatenate([p_hi, p_mid, p_lo, jnp.zeros((POS_ROWS - 9, owned), F32)], axis=0)
    near = jnp.concatenate([features, pieces.astype(BF16)], axis=0)[None]
    step = n_row // 2
    while step > 1:
        near = jnp.concatenate([near, exchange(near, "row", n_row, step)], axis=0)
        step //= 2
    far = exchange(near, "row", n_row, 1)
    col_pos = jnp.concatenate([positions, jnp.zeros((5, owned), F32)], axis=0)[None]
    step = 1
    while step < n_col:
        col_pos = jnp.concatenate([col_pos, exchange(col_pos, "col", n_col, step)], axis=0)
        step *= 2

    info = jnp.concatenate(
        [
            jnp.stack([row_index, col_index, pair_count[0, 0]]).astype(jnp.int32),
            tile_pairs[0, 0].reshape(-1),
        ]
    )

    def slot_of(s, info):
        return jnp.minimum(s, info[2] - 1)

    def chunk_of(s, c, info):
        return jnp.where(s < info[2], c, chunks - 1)

    tangent_spec = pl.BlockSpec(
        (1, CHUNK, n_feat, 2 * tile),
        lambda s, c, info: (slot_of(s, info), chunk_of(s, c, info), 0, 0),
    )
    proj_spec = pl.BlockSpec((1, n_feat, tile), lambda s, c, info: (slot_of(s, info), 0, 0))
    geom_spec = pl.BlockSpec((1, 4, half, 2 * tile), lambda s, c, info: (slot_of(s, info), 0, 0, 0))
    params = pltpu.CompilerParams(
        dimension_semantics=("arbitrary", "arbitrary"), vmem_limit_bytes=48 * 1024 * 1024
    )
    operands = (
        near, far, col_pos, masks[0, 0], w_in, w_f1, b_f1[None], w_f2, b_f2[None],
    )
    pair_plane = pltpu.VMEM((half, 2 * tile), F32)
    nbasis, hidden = w_f1.shape
    partial, tangents, proj, geom = pl.pallas_call(
        functools.partial(pair_kernel, n_row),
        grid_spec=pltpu.PrefetchScalarGridSpec(
            num_scalar_prefetch=1,
            grid=(tp, chunks),
            in_specs=[whole(x.shape) for x in operands],
            out_specs=[whole((span, n_feat)), tangent_spec, proj_spec, geom_spec],
            scratch_shapes=[
                pltpu.VMEM((2 * hidden, 2 * nbasis + 16), BF16),
                pltpu.VMEM((hidden, 2 * n_feat), F32),
                pltpu.VMEM((n_feat, n_feat), BF16),
                pltpu.VMEM((2 * tile, 2 * n_feat), BF16),
                pair_plane, pair_plane, pair_plane, pair_plane, pair_plane,
            ],
        ),
        out_shape=[
            jax.ShapeDtypeStruct((span, n_feat), F32),
            jax.ShapeDtypeStruct((tp, half, n_feat, 2 * tile), BF16),
            jax.ShapeDtypeStruct((tp, n_feat, tile), BF16),
            jax.ShapeDtypeStruct((tp, 4, half, 2 * tile), F32),
        ],
        compiler_params=params,
        name="pair_messages",
    )(info, *operands)

    step = 1
    while step < n_col // 2:
        partial = partial + exchange(partial, "col", n_col, step)
        step *= 2
    other = exchange(partial, "col", n_col, step)

    operands = (
        partial, other, features, w_o1, b_o1[None], w_o2, b_o2[None], read_w[None], w_f2, b_f2[None],
    )
    features_out, col_force, row_force = pl.pallas_call(
        functools.partial(force_kernel, n_row, tp),
        grid_spec=pltpu.PrefetchScalarGridSpec(
            num_scalar_prefetch=1,
            grid=(tp, chunks),
            in_specs=[whole(x.shape) for x in operands] + [proj_spec, geom_spec, tangent_spec],
            out_specs=[
                whole((n_feat, owned)),
                whole((n_row, 8, owned)),
                whole((n_col, 8, owned)),
            ],
            scratch_shapes=[
                pltpu.VMEM((hidden, 2 * n_feat), F32),
                pltpu.VMEM((span, n_feat), F32),
                pltpu.VMEM((span, n_feat), F32),
                pltpu.VMEM((2 * tile, 2 * n_feat), BF16),
                pair_plane, pair_plane,
            ],
        ),
        out_shape=[
            jax.ShapeDtypeStruct((n_feat, owned), BF16),
            jax.ShapeDtypeStruct((n_row, 8, owned), F32),
            jax.ShapeDtypeStruct((n_col, 8, owned), F32),
        ],
        compiler_params=params,
        name="pair_forces",
    )(info, *operands, proj, geom, tangents)

    def reduce_halves(total, axis, size):
        step = 1
        while step < size:
            keep = total.shape[0] // 2
            total = total[:keep] + exchange(total[keep:], axis, size, step)
            step *= 2
        return total[0]

    forces = reduce_halves(row_force, "col", n_col) + reduce_halves(col_force, "row", n_row)
    return (features_out, forces[:3])


def solution(mesh):
    atoms = P(None, ("row", "col"))
    in_specs = (
        atoms,
        atoms,
        P("row", "col", None, None),
        P("row", "col"),
        P("row", "col", None, None, None),
    ) + (P(),) * 10
    return jax.shard_map(
        local, mesh=mesh, in_specs=in_specs, out_specs=(atoms, atoms), check_vma=False
    )
```

```python
import functools
import math

import jax
import jax.numpy as jnp
from jax import lax
from jax.experimental import pallas as pl
from jax.experimental.pallas import tpu as pltpu
from jax.sharding import PartitionSpec as P

SOFTENING = 0.25
GAMMA_RBF = 10.0
CENTER_MAX = 10.0
CUTOFF = 12.0
LN2 = math.log(2.0)
SCALE = math.sqrt(GAMMA_RBF / LN2)
TANGENT = -GAMMA_RBF / SCALE
POS_ROWS = 16
CHUNK = 16
F32 = jnp.float32
BF16 = jnp.bfloat16


def dot(a, b):
    return jnp.dot(a, b, preferred_element_type=F32)


def dot_t(a, b):
    return lax.dot_general(a, b, (((1,), (1,)), ((), ())), preferred_element_type=F32)


def split2(x):
    hi = x.astype(BF16)
    return hi, (x - hi.astype(F32)).astype(BF16)


def fold(x):
    half = x.shape[0] // 2
    return jnp.concatenate([x[:half], x[half:]], axis=1)


def unfold(x):
    half = x.shape[1] // 2
    return jnp.concatenate([x[:, :half], x[:, half:]], axis=0)


def block_diag(x):
    zero = jnp.zeros_like(x)
    return jnp.concatenate(
        [jnp.concatenate([x, zero], axis=1), jnp.concatenate([zero, x], axis=1)], axis=0
    )


def reverse_bits(value, count):
    bits = count.bit_length() - 1
    out = jnp.int32(0)
    for k in range(bits):
        out = out | (((value >> k) & 1) << (bits - 1 - k))
    return out


def pair_kernel(
    n_row, info, near, far, col_pos, masks, w_in, w_f1, b_f1, w_f2, b_f2,
    msg, tangents, proj_out, geom_out,
    lhs, w2, w_in_t, diag, dist, coef_h, coef_x, rows, left,
):
    slot, chunk = pl.program_id(0), pl.program_id(1)
    nbasis = w_f1.shape[0]
    hidden = w_f1.shape[1]
    tile = masks.shape[-1]
    tp = masks.shape[0]

    @pl.when((slot == 0) & (chunk == 0))
    def _():
        weights = w_f1[...].astype(F32)
        zero = jnp.zeros_like(weights)
        bias = b_f1[...] * 0.5
        b_hi = bias.astype(BF16).astype(F32)
        b_mid = (bias - b_hi).astype(BF16).astype(F32)
        b_lo = bias - b_hi - b_mid
        extra = jnp.concatenate([b_hi, b_mid, b_lo, jnp.zeros((13, hidden), F32)], axis=0)
        table = jnp.concatenate(
            [
                jnp.concatenate([0.5 * weights, zero], axis=1),
                jnp.concatenate([zero, weights], axis=1),
                jnp.concatenate([extra, jnp.zeros_like(extra)], axis=1),
                jnp.zeros((256 - 2 * nbasis - 16, 2 * hidden), F32),
            ],
            axis=0,
        )
        lhs[...] = table.T[:, : 2 * nbasis + 16].astype(BF16)
        wide = w_f2[...].astype(F32)
        w2[...] = jnp.concatenate([wide, wide], axis=1)
        w_in_t[...] = w_in[...].astype(F32).T.astype(BF16)
        msg[...] = jnp.zeros_like(msg)

    @pl.when(slot < info[2])
    def _():
        @pl.when(chunk == 0)
        def _():
            row_tile, col_tile = info[3 + slot], info[3 + tp + slot]
            place = reverse_bits(col_tile ^ info[0], n_row)
            half = n_row // 2
            index = place & (half - 1)
            block = jnp.where(place >= half, far[index], near[index])
            proj = dot(w_in_t[...], block[:tile]).astype(BF16)
            proj_out[0] = proj
            proj_t = proj.astype(F32).T.astype(BF16)
            diag[...] = block_diag(proj_t)
            pieces = block[tile:].astype(F32)
            sender = pieces[0:3] + pieces[3:6] + pieces[6:9]
            receiver = col_pos[row_tile ^ info[1]]
            square = jnp.zeros((tile, tile), F32)
            separation = []
            for k in range(3):
                up = jnp.broadcast_to(receiver[k : k + 1], (tile, tile)).T
                separation.append(up - sender[k : k + 1])
                square = square + separation[k] * separation[k]
            distance = jnp.sqrt(square + SOFTENING)
            angle = (math.pi / CUTOFF) * distance
            mask = masks[slot].astype(F32)
            cut = 0.5 * (jnp.cos(angle) + 1.0) * mask
            slope = (-0.5 * math.pi / CUTOFF) * jnp.sin(angle) * mask
            dist[...] = fold(distance * SCALE)
            coef_h[...] = fold(-LN2 * cut)
            coef_x[...] = fold(
                jnp.sin(angle) / (jnp.cos(angle) + 1.0) * (LN2 * math.pi / CUTOFF / TANGENT)
            )
            geom_out[0, 4] = fold(cut * TANGENT)
            inverse = 1.0 / distance
            for k in range(3):
                geom_out[0, k] = fold(separation[k] * inverse)
            geom_out[0, 3] = fold(slope)
            c_hi, c_lo = split2(cut)
            bias_part = (dot(c_hi, proj_t) + dot(c_lo, proj_t)) * b_f2[...]
            here = pl.ds(pl.multiple_of(row_tile * tile, tile), tile)
            msg[here, :] = msg[here, :] + bias_part

        centers = lax.broadcasted_iota(jnp.int32, (nbasis, 2 * tile), 0).astype(F32) * (
            SCALE * CENTER_MAX / (nbasis - 1)
        )
        ones = jnp.ones((16, 2 * tile), BF16)
        base = pl.multiple_of(chunk * CHUNK, CHUNK)
        here = pl.ds(base, CHUNK)
        d, h, x = dist[here, :], coef_h[here, :], coef_x[here, :]
        for u in range(CHUNK):
            offset = d[u : u + 1] - centers
            gauss = jnp.exp2(-(offset * offset))
            basis = jnp.concatenate(
                [gauss.astype(BF16), (offset * gauss).astype(BF16), ones], axis=0
            )
            pre = dot(lhs[...], basis)
            bend = jnp.tanh(pre[:hidden])
            value = lax.log2(1.0 - bend)
            slope = (1.0 + bend) * pre[hidden:]
            left[pl.ds(u * hidden, hidden), :] = (h[u : u + 1] * value).astype(BF16)
            tangents[0, u] = (x[u : u + 1] * value + slope).astype(BF16)
        mixed = dot(left[...], diag[...])
        sums = [
            jnp.sum(mixed[u * hidden : (u + 1) * hidden] * w2[...], axis=0, keepdims=True)
            for u in range(CHUNK)
        ]
        rows[here, :] = jnp.concatenate(sums, axis=0)

        @pl.when(chunk == pl.num_programs(1) - 1)
        def _():
            here = pl.ds(pl.multiple_of(info[3 + slot] * tile, tile), tile)
            msg[here, :] = msg[here, :] + unfold(rows[...])


def force_kernel(
    n_row, tp, info, msg_a, msg_b, features, w_o1, b_o1, w_o2, b_o2, read_w, w_f2, b_f2, proj, geom, tangents,
    features_out, col_force, row_force,
    w2, grads, pre_act, diag, grad_rows, rows, left,
):
    slot, chunk = pl.program_id(0), pl.program_id(1)
    tile = features.shape[1]

    @pl.when((slot == 0) & (chunk == 0))
    def _():
        col_force[...] = jnp.zeros_like(col_force)
        row_force[...] = jnp.zeros_like(row_force)
        wide = w_f2[...].astype(F32)
        w2[...] = jnp.concatenate([wide, wide], axis=1)
        messages = (msg_a[...] + msg_b[...]).astype(BF16)
        pre = dot(messages, w_o1[...]) + b_o1[...]
        pre_act[...] = pre
        own = pre_act[pl.ds(pl.multiple_of(info[1] * tile, tile), tile), :]
        active = jnp.maximum(own, 0.0) + jnp.log(1.0 + jnp.exp(-jnp.abs(own))) - math.log(2.0)
        update = dot(active.astype(BF16), w_o2[...]) + b_o2[...]
        features_out[...] = (features[...].astype(F32) + update.T).astype(BF16)
        readout = jnp.broadcast_to(read_w[...], (8, tile))
        r_hi = readout.astype(BF16)
        rest = readout - r_hi.astype(F32)
        r_mid, r_lo = split2(rest)
        direction = (
            dot_t(r_hi, w_o2[...]) + (dot_t(r_mid, w_o2[...]) + dot_t(r_lo, w_o2[...]))
        )[0:1]
        s_hi, s_lo = split2(direction / (1.0 + jnp.exp(-pre)))
        grads[...] = dot_t(s_hi, w_o1[...]) + dot_t(s_lo, w_o1[...])

    @pl.when(slot < info[2])
    def _():
        @pl.when(chunk == 0)
        def _():
            here = pl.ds(pl.multiple_of(info[3 + slot] * tile, tile), tile)
            grad_rows[...] = fold(grads[here, :])
            diag[...] = block_diag(proj[0])

        here = pl.ds(pl.multiple_of(chunk * CHUNK, CHUNK), CHUNK)
        g = grad_rows[here, :]
        hidden = w2.shape[0]
        for u in range(CHUNK):
            left[pl.ds(u * hidden, hidden), :] = (w2[...] * g[u : u + 1]).astype(BF16)
        mixed = dot(left[...], diag[...])
        sums = [
            jnp.sum(
                mixed[u * hidden : (u + 1) * hidden] * tangents[0, u].astype(F32),
                axis=0,
                keepdims=True,
            )
            for u in range(CHUNK)
        ]
        rows[here, :] = jnp.concatenate(sums, axis=0)

        @pl.when(chunk == pl.num_programs(1) - 1)
        def _():
            row_tile, col_tile = info[3 + slot], info[3 + tp + slot]
            g_hi, g_lo = split2(unfold(grad_rows[...]) * b_f2[...])
            bias_part = dot(g_hi, proj[0]) + dot(g_lo, proj[0])
            dist_grad = unfold(geom[0, 4] * rows[...]) + unfold(geom[0, 3]) * bias_part
            to_rows, to_cols = [], []
            for k in range(3):
                push = unfold(geom[0, k]) * dist_grad
                to_cols.append(jnp.sum(push, axis=0, keepdims=True))
                to_rows.append(-jnp.sum(push.T, axis=0, keepdims=True))
            zero = jnp.zeros((5, tile), F32)
            place = reverse_bits(col_tile ^ info[0], n_row)
            col_force[place] = col_force[place] + jnp.concatenate(to_cols + [zero], axis=0)
            n_col = row_force.shape[0]
            place = reverse_bits(row_tile ^ info[1], n_col)
            row_force[place] = row_force[place] + jnp.concatenate(to_rows + [zero], axis=0)


def exchange(value, axis, size, step):
    return lax.ppermute(value, axis, [(i, i ^ step) for i in range(size)])


def whole(shape):
    return pl.BlockSpec(shape, lambda s, c, info: (0,) * len(shape))


def local(
    features, positions, tile_pairs, pair_count, masks,
    w_in, w_f1, b_f1, w_f2, b_f2, w_o1, b_o1, w_o2, b_o2, read_w,
):
    n_feat, owned = features.shape
    tile = masks.shape[-1]
    tp = masks.shape[2]
    n_row = lax.axis_size("row")
    n_col = lax.axis_size("col")
    row_index = lax.axis_index("row")
    col_index = lax.axis_index("col")
    span = n_col * owned
    half = tile // 2
    chunks = half // CHUNK

    p_hi = lax.reduce_precision(positions, 8, 7)
    p_mid = lax.reduce_precision(positions - p_hi, 8, 7)
    p_lo = positions - p_hi - p_mid
    pieces = jnp.concatenate([p_hi, p_mid, p_lo, jnp.zeros((POS_ROWS - 9, owned), F32)], axis=0)
    near = jnp.concatenate([features, pieces.astype(BF16)], axis=0)[None]
    step = n_row // 2
    while step > 1:
        near = jnp.concatenate([near, exchange(near, "row", n_row, step)], axis=0)
        step //= 2
    far = exchange(near, "row", n_row, 1)
    col_pos = jnp.concatenate([positions, jnp.zeros((5, owned), F32)], axis=0)[None]
    step = 1
    while step < n_col:
        col_pos = jnp.concatenate([col_pos, exchange(col_pos, "col", n_col, step)], axis=0)
        step *= 2

    info = jnp.concatenate(
        [
            jnp.stack([row_index, col_index, pair_count[0, 0]]).astype(jnp.int32),
            tile_pairs[0, 0].reshape(-1),
        ]
    )

    def slot_of(s, info):
        return jnp.minimum(s, info[2] - 1)

    def chunk_of(s, c, info):
        return jnp.where(s < info[2], c, chunks - 1)

    tangent_spec = pl.BlockSpec(
        (1, CHUNK, n_feat, 2 * tile),
        lambda s, c, info: (slot_of(s, info), chunk_of(s, c, info), 0, 0),
    )
    proj_spec = pl.BlockSpec((1, n_feat, tile), lambda s, c, info: (slot_of(s, info), 0, 0))
    geom_spec = pl.BlockSpec((1, 5, half, 2 * tile), lambda s, c, info: (slot_of(s, info), 0, 0, 0))
    params = pltpu.CompilerParams(
        dimension_semantics=("arbitrary", "arbitrary"), vmem_limit_bytes=60 * 1024 * 1024
    )
    operands = (
        near, far, col_pos, masks[0, 0], w_in, w_f1, b_f1[None], w_f2, b_f2[None],
    )
    pair_plane = pltpu.VMEM((half, 2 * tile), F32)
    nbasis, hidden = w_f1.shape
    partial, tangents, proj, geom = pl.pallas_call(
        functools.partial(pair_kernel, n_row),
        grid_spec=pltpu.PrefetchScalarGridSpec(
            num_scalar_prefetch=1,
            grid=(tp, chunks),
            in_specs=[whole(x.shape) for x in operands],
            out_specs=[whole((span, n_feat)), tangent_spec, proj_spec, geom_spec],
            scratch_shapes=[
                pltpu.VMEM((2 * hidden, 2 * nbasis + 16), BF16),
                pltpu.VMEM((hidden, 2 * n_feat), F32),
                pltpu.VMEM((n_feat, n_feat), BF16),
                pltpu.VMEM((2 * tile, 2 * n_feat), BF16),
                pair_plane, pair_plane, pair_plane, pair_plane,
                pltpu.VMEM((CHUNK * hidden, 2 * tile), BF16),
            ],
        ),
        out_shape=[
            jax.ShapeDtypeStruct((span, n_feat), F32),
            jax.ShapeDtypeStruct((tp, half, n_feat, 2 * tile), BF16),
            jax.ShapeDtypeStruct((tp, n_feat, tile), BF16),
            jax.ShapeDtypeStruct((tp, 5, half, 2 * tile), F32),
        ],
        compiler_params=params,
        name="pair_messages",
    )(info, *operands)

    step = 1
    while step < n_col // 2:
        partial = partial + exchange(partial, "col", n_col, step)
        step *= 2
    other = exchange(partial, "col", n_col, step)

    operands = (
        partial, other, features, w_o1, b_o1[None], w_o2, b_o2[None], read_w[None], w_f2, b_f2[None],
    )
    features_out, col_force, row_force = pl.pallas_call(
        functools.partial(force_kernel, n_row, tp),
        grid_spec=pltpu.PrefetchScalarGridSpec(
            num_scalar_prefetch=1,
            grid=(tp, chunks),
            in_specs=[whole(x.shape) for x in operands] + [proj_spec, geom_spec, tangent_spec],
            out_specs=[
                whole((n_feat, owned)),
                whole((n_row, 8, owned)),
                whole((n_col, 8, owned)),
            ],
            scratch_shapes=[
                pltpu.VMEM((hidden, 2 * n_feat), F32),
                pltpu.VMEM((span, n_feat), F32),
                pltpu.VMEM((span, n_feat), F32),
                pltpu.VMEM((2 * tile, 2 * n_feat), BF16),
                pair_plane, pair_plane,
                pltpu.VMEM((CHUNK * hidden, 2 * n_feat), BF16),
            ],
        ),
        out_shape=[
            jax.ShapeDtypeStruct((n_feat, owned), BF16),
            jax.ShapeDtypeStruct((n_row, 8, owned), F32),
            jax.ShapeDtypeStruct((n_col, 8, owned), F32),
        ],
        compiler_params=params,
        name="pair_forces",
    )(info, *operands, proj, geom, tangents)

    def reduce_halves(total, axis, size):
        step = 1
        while step < size:
            keep = total.shape[0] // 2
            total = total[:keep] + exchange(total[keep:], axis, size, step)
            step *= 2
        return total[0]

    forces = reduce_halves(row_force, "col", n_col) + reduce_halves(col_force, "row", n_row)
    return (features_out, forces[:3])


def solution(mesh):
    atoms = P(None, ("row", "col"))
    in_specs = (
        atoms,
        atoms,
        P("row", "col", None, None),
        P("row", "col"),
        P("row", "col", None, None, None),
    ) + (P(),) * 10
    return jax.shard_map(
        local, mesh=mesh, in_specs=in_specs, out_specs=(atoms, atoms), check_vma=False
    )
```

```python
import math

import jax
import jax.numpy as jnp
from jax import lax
from jax.experimental import pallas as pl
from jax.experimental.pallas import tpu as pltpu
from jax.sharding import PartitionSpec as P

SOFTENING = 0.25
GAMMA_RBF = 10.0
CENTER_MAX = 10.0
CUTOFF = 12.0
LN2 = math.log(2.0)
SCALE = math.sqrt(GAMMA_RBF / LN2)
TANGENT = -GAMMA_RBF / SCALE
POS_ROWS = 16
CHUNK = 16
MIB = 1024 * 1024
F32 = jnp.float32
BF16 = jnp.bfloat16


def dot(a, b):
    return jnp.dot(a, b, preferred_element_type=F32)


def dot_t(a, b):
    return lax.dot_general(a, b, (((1,), (1,)), ((), ())), preferred_element_type=F32)


def split2(x):
    hi = x.astype(BF16)
    return hi, (x - hi.astype(F32)).astype(BF16)


def fold(x):
    half = x.shape[0] // 2
    return jnp.concatenate([x[:half], x[half:]], axis=1)


def unfold(x):
    half = x.shape[1] // 2
    return jnp.concatenate([x[:, :half], x[:, half:]], axis=0)


def block_diag(x):
    zero = jnp.zeros_like(x)
    return jnp.concatenate(
        [jnp.concatenate([x, zero], axis=1), jnp.concatenate([zero, x], axis=1)], axis=0
    )


def reverse_bits(value, count):
    bits = count.bit_length() - 1
    out = jnp.int32(0)
    for k in range(bits):
        out = out | (((value >> k) & 1) << (bits - 1 - k))
    return out


def out_type(shape, dtype):
    return pltpu.VMEM(shape, dtype)


def fetch(sources, targets, sems):
    copies = [
        pltpu.make_async_copy(src, dst, sems.at[k])
        for k, (src, dst) in enumerate(zip(sources, targets))
    ]
    for copy in copies:
        copy.start()
    for copy in copies:
        copy.wait()


def pack_kernel(features_hbm, positions_hbm, out, col_pos, features, positions, sems):
    fetch([features_hbm, positions_hbm], [features, positions], sems)
    n_feat = features.shape[0]
    col_pos[0] = jnp.concatenate([positions[...], jnp.zeros((5, positions.shape[1]), F32)], axis=0)
    out[0, :n_feat] = features[...]
    exact = positions[...]
    hi = exact.astype(BF16).astype(F32)
    mid = (exact - hi).astype(BF16).astype(F32)
    pad = jnp.zeros((POS_ROWS - 9, exact.shape[1]), F32)
    pieces = jnp.concatenate([hi, mid, exact - hi - mid, pad], axis=0)
    out[0, n_feat:] = pieces.astype(BF16)


def weight_kernel(
    w_in_hbm, w_f1_hbm, b_f1_hbm, w_f2_hbm, read_w_hbm, w_o2_hbm, w_o1_hbm, b_f2_hbm, b_o1_hbm, b_o2_hbm, masks_hbm,
    lhs, w2, w_in_t, direction, w_o2, w_o1, b_f2, b_o1, b_o2, masks,
    w_in, w_f1, b_f1, w_f2, read_w, sems,
):
    fetch(
        [
            w_in_hbm, w_f1_hbm, b_f1_hbm, w_f2_hbm, read_w_hbm, w_o2_hbm,
            w_o1_hbm, b_f2_hbm, b_o1_hbm, b_o2_hbm, masks_hbm,
        ],
        [w_in, w_f1, b_f1, w_f2, read_w, w_o2, w_o1, b_f2, b_o1, b_o2, masks],
        sems,
    )
    nbasis, hidden = w_f1.shape
    weights = w_f1[...].astype(F32)
    zero = jnp.zeros_like(weights)
    bias = b_f1[...] * 0.5
    b_hi = bias.astype(BF16).astype(F32)
    b_mid = (bias - b_hi).astype(BF16).astype(F32)
    b_lo = bias - b_hi - b_mid
    extra = jnp.concatenate([b_hi, b_mid, b_lo, jnp.zeros((13, hidden), F32)], axis=0)
    table = jnp.concatenate(
        [
            jnp.concatenate([0.5 * weights, zero], axis=1),
            jnp.concatenate([zero, weights], axis=1),
            jnp.concatenate([extra, jnp.zeros_like(extra)], axis=1),
            jnp.zeros((256 - 2 * nbasis - 16, 2 * hidden), F32),
        ],
        axis=0,
    )
    lhs[...] = table.T[:, : 2 * nbasis + 16].astype(BF16)
    wide = w_f2[...].astype(F32)
    w2[...] = jnp.concatenate([wide, wide], axis=1)
    w_in_t[...] = w_in[...].astype(F32).T.astype(BF16)
    readout = jnp.broadcast_to(read_w[...], (8, read_w.shape[1]))
    r_hi = readout.astype(BF16)
    r_mid, r_lo = split2(readout - r_hi.astype(F32))
    direction[...] = dot_t(r_hi, w_o2[...]) + (dot_t(r_mid, w_o2[...]) + dot_t(r_lo, w_o2[...]))


def pair_kernel(
    count, pairs, near, far, col_pos, masks, lhs, w2, w_in_t, b_f2,
    msg, tangents, proj_out, geom_out,
    diag, dist, coef_h, coef_x, rows, left,
):
    n_row = lax.axis_size("row")
    me_row = lax.axis_index("row")
    me_col = lax.axis_index("col")
    tile = masks.shape[2]
    hidden = w2.shape[0]
    nbasis = (lhs.shape[1] - 16) // 2
    msg[...] = jnp.zeros_like(msg)
    centers = lax.broadcasted_iota(jnp.int32, (nbasis, 2 * tile), 0).astype(F32) * (
        SCALE * CENTER_MAX / (nbasis - 1)
    )
    ones = jnp.ones((16, 2 * tile), BF16)

    @pl.loop(0, count[0, 0])
    def _(slot):
        row_tile, col_tile = pairs[0, 0, 0, slot], pairs[0, 0, 1, slot]
        place = reverse_bits(col_tile ^ me_row, n_row)
        half = n_row // 2
        index = place & (half - 1)
        block = jnp.where(place >= half, far[index], near[index])
        proj = dot(w_in_t[...], block[:tile]).astype(BF16)
        proj_out[slot] = proj
        proj_t = proj.astype(F32).T.astype(BF16)
        diag[...] = block_diag(proj_t)
        pieces = block[tile:].astype(F32)
        sender = pieces[0:3] + pieces[3:6] + pieces[6:9]
        receiver = col_pos[row_tile ^ me_col]
        square = jnp.zeros((tile, tile), F32)
        separation = []
        for k in range(3):
            up = jnp.broadcast_to(receiver[k : k + 1], (tile, tile)).T
            separation.append(up - sender[k : k + 1])
            square = square + separation[k] * separation[k]
        distance = jnp.sqrt(square + SOFTENING)
        angle = (math.pi / CUTOFF) * distance
        mask = masks[slot].astype(F32)
        cosine, sine = jnp.cos(angle), jnp.sin(angle)
        cut = 0.5 * (cosine + 1.0) * mask
        dist[...] = fold(distance * SCALE)
        coef_h[...] = fold(-LN2 * cut)
        coef_x[...] = fold(sine / (cosine + 1.0) * (LN2 * math.pi / CUTOFF / TANGENT))
        inverse = 1.0 / distance
        for k in range(3):
            geom_out[slot, k] = fold(separation[k] * inverse)
        geom_out[slot, 3] = fold((-0.5 * math.pi / CUTOFF) * sine * mask)
        geom_out[slot, 4] = fold(cut * TANGENT)
        c_hi, c_lo = split2(cut)
        bias_part = (dot(c_hi, proj_t) + dot(c_lo, proj_t)) * b_f2[...]

        @pl.loop(0, tile // 2 // CHUNK)
        def _(chunk):
            base = pl.multiple_of(chunk * CHUNK, CHUNK)
            here = pl.ds(base, CHUNK)
            d, h, x = dist[here, :], coef_h[here, :], coef_x[here, :]
            for u in range(CHUNK):
                offset = d[u : u + 1] - centers
                gauss = jnp.exp2(-(offset * offset))
                basis = jnp.concatenate(
                    [gauss.astype(BF16), (offset * gauss).astype(BF16), ones], axis=0
                )
                pre = dot(lhs[...], basis)
                bend = jnp.tanh(pre[:hidden])
                value = lax.log2(1.0 - bend)
                slope = (1.0 + bend) * pre[hidden:]
                left[pl.ds(u * hidden, hidden), :] = (h[u : u + 1] * value).astype(BF16)
                tangents[slot, base + u] = (x[u : u + 1] * value + slope).astype(BF16)
            mixed = dot(left[...], diag[...])
            sums = [
                jnp.sum(mixed[u * hidden : (u + 1) * hidden] * w2[...], axis=0, keepdims=True)
                for u in range(CHUNK)
            ]
            rows[here, :] = jnp.concatenate(sums, axis=0)

        here = pl.ds(pl.multiple_of(row_tile * tile, tile), tile)
        msg[here, :] = msg[here, :] + (bias_part + unfold(rows[...]))


def force_kernel(
    count, pairs, msg_a, msg_b, near, w_o1, b_o1, w_o2, b_o2, direction, w2, b_f2,
    proj, geom, tangents,
    features_out, keep, send, row_keep, row_send,
    grads, pre_act, diag, rows, left, force, row_force,
):
    n_row = lax.axis_size("row")
    n_col = lax.axis_size("col")
    me_row = lax.axis_index("row")
    me_col = lax.axis_index("col")
    n_feat, tile = features_out.shape
    hidden = w2.shape[0]
    force[...] = jnp.zeros_like(force)
    row_force[...] = jnp.zeros_like(row_force)
    messages = (msg_a[...] + msg_b[...]).astype(BF16)
    pre = dot(messages, w_o1[...]) + b_o1[...]
    pre_act[...] = pre
    s_hi, s_lo = split2(direction[0:1] / (1.0 + jnp.exp(-pre)))
    grads[...] = dot_t(s_hi, w_o1[...]) + dot_t(s_lo, w_o1[...])
    own = pre_act[pl.ds(pl.multiple_of(me_col * tile, tile), tile), :]
    active = jnp.maximum(own, 0.0) + jnp.log(1.0 + jnp.exp(-jnp.abs(own))) - LN2
    update = dot(active.astype(BF16), w_o2[...]) + b_o2[...]
    features_out[...] = (near[0, :n_feat].astype(F32) + update.T).astype(BF16)

    @pl.loop(0, count[0, 0])
    def _(slot):
        row_tile, col_tile = pairs[0, 0, 0, slot], pairs[0, 0, 1, slot]
        here = pl.ds(pl.multiple_of(row_tile * tile, tile), tile)
        grad_rows = grads[here, :]
        left_rows = fold(grad_rows)
        rows[...] = left_rows
        diag[...] = block_diag(proj[slot])

        @pl.loop(0, tile // 2 // CHUNK)
        def _(chunk):
            base = pl.multiple_of(chunk * CHUNK, CHUNK)
            here = pl.ds(base, CHUNK)
            g = rows[here, :]
            for u in range(CHUNK):
                left[pl.ds(u * hidden, hidden), :] = (w2[...] * g[u : u + 1]).astype(BF16)
            mixed = dot(left[...], diag[...])
            sums = [
                jnp.sum(
                    mixed[u * hidden : (u + 1) * hidden] * tangents[slot, base + u].astype(F32),
                    axis=0,
                    keepdims=True,
                )
                for u in range(CHUNK)
            ]
            rows[here, :] = jnp.concatenate(sums, axis=0)

        g_hi, g_lo = split2(grad_rows * b_f2[...])
        bias_part = dot(g_hi, proj[slot]) + dot(g_lo, proj[slot])
        dist_grad = unfold(geom[slot, 4] * rows[...]) + unfold(geom[slot, 3]) * bias_part
        to_rows, to_cols = [], []
        for k in range(3):
            push = unfold(geom[slot, k]) * dist_grad
            to_cols.append(jnp.sum(push, axis=0, keepdims=True))
            to_rows.append(-jnp.sum(push.T, axis=0, keepdims=True))
        zero = jnp.zeros((5, tile), F32)
        place = reverse_bits(col_tile ^ me_row, n_row)
        force[place] = force[place] + jnp.concatenate(to_cols + [zero], axis=0)
        place = reverse_bits(row_tile ^ me_col, n_col)
        row_force[place] = row_force[place] + jnp.concatenate(to_rows + [zero], axis=0)

    keep[...] = force[: n_row // 2]
    send[...] = force[n_row // 2 :]
    row_keep[...] = row_force[: n_col // 2]
    row_send[...] = row_force[n_col // 2 :]


def exchange(value, axis, size, step):
    return lax.ppermute(value, axis, [(i, i ^ step) for i in range(size)])


SMEM = pl.BlockSpec(memory_space=pltpu.SMEM)
VMEM = pl.BlockSpec(memory_space=pltpu.VMEM)
HBM = pl.BlockSpec(memory_space=pltpu.HBM)


def run(kernel, name, specs, out_shape, scratch, limit, *operands):
    return pl.pallas_call(
        kernel,
        in_specs=specs,
        out_specs=jax.tree.map(lambda _: VMEM, out_shape),
        out_shape=out_shape,
        scratch_shapes=scratch,
        compiler_params=pltpu.CompilerParams(vmem_limit_bytes=limit * MIB),
        name=name,
    )(*operands)


def local(
    features, positions, tile_pairs, pair_count, masks,
    w_in, w_f1, b_f1, w_f2, b_f2, w_o1, b_o1, w_o2, b_o2, read_w,
):
    n_feat, owned = features.shape
    tile = masks.shape[-1]
    tp = masks.shape[2]
    n_row = lax.axis_size("row")
    n_col = lax.axis_size("col")
    span = n_col * owned
    half = tile // 2
    nbasis, hidden = w_f1.shape

    near, col_pos = run(
        pack_kernel, "pack_tile", [HBM, HBM],
        [out_type((1, n_feat + POS_ROWS, owned), BF16), out_type((1, 8, owned), F32)],
        [
            pltpu.VMEM(features.shape, BF16),
            pltpu.VMEM(positions.shape, F32),
            pltpu.SemaphoreType.DMA((2,)),
        ],
        60,
        features, positions,
    )
    lhs, w2, w_in_t, direction, w_o2, w_o1, b_f2, b_o1, b_o2, masks = run(
        weight_kernel, "weight_tables", [HBM] * 11,
        [
            out_type((2 * hidden, 2 * nbasis + 16), BF16),
            out_type((hidden, 2 * n_feat), F32),
            out_type((n_feat, n_feat), BF16),
            out_type((8, n_feat), F32),
            out_type(w_o2.shape, BF16),
            out_type(w_o1.shape, BF16),
        ]
        + [out_type((1, n_feat), F32)] * 3
        + [out_type((tp, tile, tile), jnp.int32)],
        [
            pltpu.VMEM(w_in.shape, BF16),
            pltpu.VMEM(w_f1.shape, BF16),
            pltpu.VMEM((1, hidden), F32),
            pltpu.VMEM(w_f2.shape, BF16),
            pltpu.VMEM((1, n_feat), F32),
            pltpu.SemaphoreType.DMA((11,)),
        ],
        60,
        w_in, w_f1, b_f1[None], w_f2, read_w[None], w_o2, w_o1, b_f2[None], b_o1[None], b_o2[None],
        masks[0, 0],
    )
    step = n_row // 2
    while step > 1:
        near = jnp.concatenate([near, exchange(near, "row", n_row, step)], axis=0)
        step //= 2
    far = exchange(near, "row", n_row, 1)
    step = 1
    while step < n_col:
        col_pos = jnp.concatenate([col_pos, exchange(col_pos, "col", n_col, step)], axis=0)
        step *= 2
    count, pairs = pair_count, tile_pairs

    plane = pltpu.VMEM((half, 2 * tile), F32)
    partial, tangents, proj, geom = run(
        pair_kernel, "pair_messages", [SMEM, SMEM] + [VMEM] * 8,
        [
            out_type((span, n_feat), F32),
            out_type((tp, half, n_feat, 2 * tile), BF16),
            out_type((tp, n_feat, tile), BF16),
            out_type((tp, 5, half, 2 * tile), F32),
        ],
        [
            pltpu.VMEM((2 * tile, 2 * n_feat), BF16),
            plane, plane, plane, plane,
            pltpu.VMEM((CHUNK * hidden, 2 * tile), BF16),
        ],
        16,
        count, pairs, near, far, col_pos, masks, lhs, w2, w_in_t, b_f2,
    )

    step = 1
    while step < n_col // 2:
        partial = partial + exchange(partial, "col", n_col, step)
        step *= 2
    other = exchange(partial, "col", n_col, step)

    features_out, keep, send, row_keep, row_send = run(
        force_kernel, "pair_forces",
        [SMEM, SMEM] + [VMEM] * 13,
        [
            out_type((n_feat, owned), BF16),
            out_type((n_row // 2, 8, owned), F32),
            out_type((n_row // 2, 8, owned), F32),
            out_type((n_col // 2, 8, owned), F32),
            out_type((n_col // 2, 8, owned), F32),
        ],
        [
            pltpu.VMEM((span, n_feat), F32),
            pltpu.VMEM((span, n_feat), F32),
            pltpu.VMEM((2 * tile, 2 * n_feat), BF16),
            plane,
            pltpu.VMEM((CHUNK * hidden, 2 * n_feat), BF16),
            pltpu.VMEM((n_row, 8, owned), F32),
            pltpu.VMEM((n_col, 8, owned), F32),
        ],
        16,
        count, pairs, partial, other, near, w_o1, b_o1, w_o2, b_o2, direction, w2, b_f2,
        proj, geom, tangents,
    )

    def reduce_halves(keep, send, axis, size):
        step = 1
        while True:
            other = exchange(send, axis, size, step)
            half = keep.shape[0] // 2
            step *= 2
            if step == size:
                return (keep + other)[0]
            send = keep[half:] + other[half:]
            keep = keep[:half] + other[:half]

    forces = reduce_halves(keep, send, "row", n_row) + reduce_halves(
        row_keep, row_send, "col", n_col
    )
    return (features_out, forces[:3])


def solution(mesh):
    atoms = P(None, ("row", "col"))
    in_specs = (
        atoms,
        atoms,
        P("row", "col", None, None),
        P("row", "col"),
        P("row", "col", None, None, None),
    ) + (P(),) * 10
    return jax.shard_map(
        local, mesh=mesh, in_specs=in_specs, out_specs=(atoms, atoms), check_vma=False
    )
```

```python
import math

import jax
import jax.numpy as jnp
from jax import lax
from jax.experimental import pallas as pl
from jax.experimental.pallas import tpu as pltpu
from jax.sharding import PartitionSpec as P

SOFTENING = 0.25
GAMMA_RBF = 10.0
CENTER_MAX = 10.0
CUTOFF = 12.0
LN2 = math.log(2.0)
SCALE = math.sqrt(GAMMA_RBF / LN2)
TANGENT = -GAMMA_RBF / SCALE
POS_ROWS = 16
CHUNK = 16
MIB = 1024 * 1024
F32 = jnp.float32
BF16 = jnp.bfloat16


def dot(a, b):
    return jnp.dot(a, b, preferred_element_type=F32)


def dot_t(a, b):
    return lax.dot_general(a, b, (((1,), (1,)), ((), ())), preferred_element_type=F32)


def split2(x):
    hi = x.astype(BF16)
    return hi, (x - hi.astype(F32)).astype(BF16)


def fold(x):
    half = x.shape[0] // 2
    return jnp.concatenate([x[:half], x[half:]], axis=1)


def unfold(x):
    half = x.shape[1] // 2
    return jnp.concatenate([x[:, :half], x[:, half:]], axis=0)


def block_diag(x):
    zero = jnp.zeros_like(x)
    return jnp.concatenate(
        [jnp.concatenate([x, zero], axis=1), jnp.concatenate([zero, x], axis=1)], axis=0
    )


def reverse_bits(value, count):
    bits = count.bit_length() - 1
    out = jnp.int32(0)
    for k in range(bits):
        out = out | (((value >> k) & 1) << (bits - 1 - k))
    return out


def out_type(shape, dtype):
    return pltpu.VMEM(shape, dtype)


def spread(row, count):
    rows = jnp.broadcast_to(row, (16, row.shape[1])).astype(BF16)
    return jnp.concatenate([rows] * (count // 16), axis=0)


def sin_cos(angle):
    turn = angle - 0.5 * math.pi
    square = turn * turn
    odd, even = 0.0, 0.0
    for k in range(6, -1, -1):
        odd = odd * square + (-1.0) ** k / math.factorial(2 * k + 1)
        even = even * square + (-1.0) ** k / math.factorial(2 * k)
    return even, -(odd * turn)


def fetch(sources, targets, sems):
    copies = [
        pltpu.make_async_copy(src, dst, sems.at[k])
        for k, (src, dst) in enumerate(zip(sources, targets))
    ]
    for copy in copies:
        copy.start()
    for copy in copies:
        copy.wait()


def pack_kernel(features_hbm, positions_hbm, out, col_pos, features, positions, sems):
    fetch([features_hbm, positions_hbm], [features, positions], sems)
    n_feat = features.shape[0]
    col_pos[0] = jnp.concatenate([positions[...], jnp.zeros((5, positions.shape[1]), F32)], axis=0)
    out[0, :n_feat] = features[...]
    exact = positions[...]
    hi = exact.astype(BF16).astype(F32)
    mid = (exact - hi).astype(BF16).astype(F32)
    pad = jnp.zeros((POS_ROWS - 9, exact.shape[1]), F32)
    pieces = jnp.concatenate([hi, mid, exact - hi - mid, pad], axis=0)
    out[0, n_feat:] = pieces.astype(BF16)


def stack_kernel(held, got, *rest):
    out = rest[-1]
    out[: held.shape[0]] = held[...]
    out[held.shape[0] :] = got[...]


def weight_kernel(
    w_in_hbm, w_f1_hbm, b_f1_hbm, w_f2_hbm, read_w_hbm, w_o2_hbm, w_o1_hbm, b_f2_hbm, b_o1_hbm, b_o2_hbm, masks_hbm, pairs_hbm,
    lhs, w2, w2_16, w_in_t, direction, w_o2, w_o1, b_f2, b_o1, b_o2, masks, pairs,
    w_in, w_f1, b_f1, w_f2, read_w, sems,
):
    fetch(
        [
            w_in_hbm, w_f1_hbm, b_f1_hbm, w_f2_hbm, read_w_hbm, w_o2_hbm,
            w_o1_hbm, b_f2_hbm, b_o1_hbm, b_o2_hbm, masks_hbm, pairs_hbm,
        ],
        [w_in, w_f1, b_f1, w_f2, read_w, w_o2, w_o1, b_f2, b_o1, b_o2, masks, pairs],
        sems,
    )
    nbasis, hidden = w_f1.shape
    weights = w_f1[...].astype(F32)
    zero = jnp.zeros_like(weights)
    bias = b_f1[...] * 0.5
    b_hi = bias.astype(BF16).astype(F32)
    b_mid = (bias - b_hi).astype(BF16).astype(F32)
    b_lo = bias - b_hi - b_mid
    extra = jnp.concatenate([b_hi, b_mid, b_lo, jnp.zeros((13, hidden), F32)], axis=0)
    table = jnp.concatenate(
        [
            jnp.concatenate([0.5 * weights, zero], axis=1),
            jnp.concatenate([zero, weights], axis=1),
            jnp.concatenate([extra, jnp.zeros_like(extra)], axis=1),
            jnp.zeros((256 - 2 * nbasis - 16, 2 * hidden), F32),
        ],
        axis=0,
    )
    lhs[...] = table.T[:, : 2 * nbasis + 16].astype(BF16)
    wide = w_f2[...].astype(F32)
    w2[...] = jnp.concatenate([wide, wide], axis=1)
    w2_16[...] = w2[...].astype(BF16)
    w_in_t[...] = w_in[...].astype(F32).T.astype(BF16)
    readout = jnp.broadcast_to(read_w[...], (8, read_w.shape[1]))
    r_hi = readout.astype(BF16)
    r_mid, r_lo = split2(readout - r_hi.astype(F32))
    direction[...] = dot_t(r_hi, w_o2[...]) + (dot_t(r_mid, w_o2[...]) + dot_t(r_lo, w_o2[...]))


def pair_kernel(
    count, pairs, near, far, col_pos, masks, lhs, w2, w_in_t, b_f2,
    msg, msg16, tangents, proj_out, geom_out,
    diag, dist, coef_h, coef_x, rows, left,
):
    n_row = lax.axis_size("row")
    me_row = lax.axis_index("row")
    me_col = lax.axis_index("col")
    tile = masks.shape[2]
    hidden = w2.shape[0]
    nbasis = (lhs.shape[1] - 16) // 2
    msg[...] = jnp.zeros_like(msg)
    centers = lax.broadcasted_iota(jnp.int32, (nbasis, 2 * tile), 0).astype(F32) * (
        SCALE * CENTER_MAX / (nbasis - 1)
    )
    ones = jnp.ones((16, 2 * tile), BF16)

    @pl.loop(0, count[0, 0])
    def _(slot):
        row_tile, col_tile = pairs[0, 0, 0, slot], pairs[0, 0, 1, slot]
        place = reverse_bits(col_tile ^ me_row, n_row)
        half = n_row // 2
        index = place & (half - 1)
        block = jnp.where(place >= half, far[index], near[index])
        proj = dot(w_in_t[...], block[:tile]).astype(BF16)
        proj_out[slot] = proj
        proj_t = proj.astype(F32).T.astype(BF16)
        diag[...] = block_diag(proj_t)
        pieces = block[tile:].astype(F32)
        sender = pieces[0:3] + pieces[3:6] + pieces[6:9]
        receiver = col_pos[row_tile ^ me_col]
        square = jnp.zeros((tile, tile), F32)
        separation = []
        for k in range(3):
            up = jnp.broadcast_to(receiver[k : k + 1], (tile, tile)).T
            separation.append(up - sender[k : k + 1])
            square = square + separation[k] * separation[k]
        distance = jnp.sqrt(square + SOFTENING)
        angle = (math.pi / CUTOFF) * distance
        mask = masks[slot].astype(F32)
        sine, cosine = sin_cos(angle)
        cut = 0.5 * (cosine + 1.0) * mask
        dist[...] = fold(distance * SCALE)
        coef_h[...] = fold(-LN2 * cut)
        coef_x[...] = fold(sine / (cosine + 1.0) * (LN2 * math.pi / CUTOFF / TANGENT))
        inverse = 1.0 / distance
        for k in range(3):
            geom_out[slot, k] = fold(separation[k] * inverse)
        geom_out[slot, 3] = fold((-0.5 * math.pi / CUTOFF) * sine * mask)
        geom_out[slot, 4] = fold(cut * TANGENT)
        c_hi, c_lo = split2(cut)
        bias_part = (dot(c_hi, proj_t) + dot(c_lo, proj_t)) * b_f2[...]

        @pl.loop(0, tile // 2 // CHUNK)
        def _(chunk):
            base = pl.multiple_of(chunk * CHUNK, CHUNK)
            here = pl.ds(base, CHUNK)
            d, h, x = dist[here, :], coef_h[here, :], coef_x[here, :]
            for u in range(CHUNK):
                offset = d[u : u + 1] - centers
                gauss = jnp.exp2(-(offset * offset))
                basis = jnp.concatenate(
                    [gauss.astype(BF16), (offset * gauss).astype(BF16), ones], axis=0
                )
                pre = dot(lhs[...], basis)
                bend = jnp.tanh(pre[:hidden])
                value = lax.log2(1.0 - bend)
                slope = (1.0 + bend) * pre[hidden:]
                value = value.astype(BF16)
                left[pl.ds(u * hidden, hidden), :] = spread(h[u : u + 1], hidden) * value
                tangents[slot, base + u] = spread(x[u : u + 1], hidden) * value + slope.astype(BF16)
            mixed = dot(left[...], diag[...])
            sums = [
                jnp.sum(mixed[u * hidden : (u + 1) * hidden] * w2[...], axis=0, keepdims=True)
                for u in range(CHUNK)
            ]
            rows[here, :] = jnp.concatenate(sums, axis=0)

        here = pl.ds(pl.multiple_of(row_tile * tile, tile), tile)
        msg[here, :] = msg[here, :] + (bias_part + unfold(rows[...]))

    msg16[...] = msg[...].astype(BF16)


def force_kernel(
    count, pairs, msg_a, msg_b, near, w_o1, b_o1, w_o2, b_o2, direction, w2_16, b_f2,
    proj, geom, tangents,
    features_hbm, keep, send, row_keep, row_send,
    features_out, grads, pre_act, diag, rows, left, force, row_force, sems,
):
    n_row = lax.axis_size("row")
    n_col = lax.axis_size("col")
    me_row = lax.axis_index("row")
    me_col = lax.axis_index("col")
    n_feat, tile = features_out.shape
    hidden = w2_16.shape[0]
    force[...] = jnp.zeros_like(force)
    row_force[...] = jnp.zeros_like(row_force)
    messages = (msg_a[...] + msg_b[...].astype(F32)).astype(BF16)
    pre = dot(messages, w_o1[...]) + b_o1[...]
    pre_act[...] = pre
    s_hi, s_lo = split2(direction[0:1] / (1.0 + jnp.exp(-pre)))
    grads[...] = dot_t(s_hi, w_o1[...]) + dot_t(s_lo, w_o1[...])
    own = pre_act[pl.ds(pl.multiple_of(me_col * tile, tile), tile), :]
    active = jnp.maximum(own, 0.0) + jnp.log(1.0 + jnp.exp(-jnp.abs(own))) - LN2
    update = dot(active.astype(BF16), w_o2[...]) + b_o2[...]
    features_out[...] = (near[0, :n_feat].astype(F32) + update.T).astype(BF16)
    store = pltpu.make_async_copy(features_out, features_hbm, sems.at[0])
    store.start()

    @pl.loop(0, count[0, 0])
    def _(slot):
        row_tile, col_tile = pairs[0, 0, 0, slot], pairs[0, 0, 1, slot]
        here = pl.ds(pl.multiple_of(row_tile * tile, tile), tile)
        grad_rows = grads[here, :]
        left_rows = fold(grad_rows)
        rows[...] = left_rows
        diag[...] = block_diag(proj[slot])

        @pl.loop(0, tile // 2 // CHUNK)
        def _(chunk):
            base = pl.multiple_of(chunk * CHUNK, CHUNK)
            here = pl.ds(base, CHUNK)
            g = rows[here, :]
            for u in range(CHUNK):
                left[pl.ds(u * hidden, hidden), :] = w2_16[...] * spread(g[u : u + 1], hidden)
            mixed = dot(left[...], diag[...])
            sums = [
                jnp.sum(
                    mixed[u * hidden : (u + 1) * hidden] * tangents[slot, base + u].astype(F32),
                    axis=0,
                    keepdims=True,
                )
                for u in range(CHUNK)
            ]
            rows[here, :] = jnp.concatenate(sums, axis=0)

        g_hi, g_lo = split2(grad_rows * b_f2[...])
        bias_part = dot(g_hi, proj[slot]) + dot(g_lo, proj[slot])
        dist_grad = unfold(geom[slot, 4] * rows[...]) + unfold(geom[slot, 3]) * bias_part
        to_rows, to_cols = [], []
        for k in range(3):
            push = unfold(geom[slot, k]) * dist_grad
            to_cols.append(jnp.sum(push, axis=0, keepdims=True))
            to_rows.append(-jnp.sum(push.T, axis=0, keepdims=True))
        zero = jnp.zeros((5, tile), F32)
        place = reverse_bits(col_tile ^ me_row, n_row)
        force[place] = force[place] + jnp.concatenate(to_cols + [zero], axis=0)
        place = reverse_bits(row_tile ^ me_col, n_col)
        row_force[place] = row_force[place] + jnp.concatenate(to_rows + [zero], axis=0)

    keep[...] = force[: n_row // 2]
    send[...] = force[n_row // 2 :]
    row_keep[...] = row_force[: n_col // 2]
    row_send[...] = row_force[n_col // 2 :]
    store.wait()


def exchange(value, axis, size, step):
    return lax.ppermute(value, axis, [(i, i ^ step) for i in range(size)])


ANY = pl.BlockSpec(memory_space=pl.ANY)
SMEM = pl.BlockSpec(memory_space=pltpu.SMEM)
VMEM = pl.BlockSpec(memory_space=pltpu.VMEM)
HBM = pl.BlockSpec(memory_space=pltpu.HBM)


def run(kernel, name, specs, out_shape, scratch, limit, *operands):
    return pl.pallas_call(
        kernel,
        in_specs=specs,
        out_specs=[pl.BlockSpec(memory_space=x.memory_space) for x in out_shape],
        out_shape=out_shape,
        scratch_shapes=scratch,
        compiler_params=pltpu.CompilerParams(vmem_limit_bytes=limit * MIB),
        name=name,
    )(*operands)


def local(
    features, positions, tile_pairs, pair_count, masks,
    w_in, w_f1, b_f1, w_f2, b_f2, w_o1, b_o1, w_o2, b_o2, read_w,
):
    n_feat, owned = features.shape
    tile = masks.shape[-1]
    tp = masks.shape[2]
    n_row = lax.axis_size("row")
    n_col = lax.axis_size("col")
    span = n_col * owned
    half = tile // 2
    nbasis, hidden = w_f1.shape

    near, col_pos = run(
        pack_kernel, "pack_tile", [HBM, HBM],
        [out_type((1, n_feat + POS_ROWS, owned), BF16), out_type((1, 8, owned), F32)],
        [
            pltpu.VMEM(features.shape, BF16),
            pltpu.VMEM(positions.shape, F32),
            pltpu.SemaphoreType.DMA((2,)),
        ],
        60,
        features, positions,
    )
    lhs, w2, w2_16, w_in_t, direction, w_o2, w_o1, b_f2, b_o1, b_o2, masks, pairs = run(
        weight_kernel, "weight_tables", [HBM] * 12,
        [
            out_type((2 * hidden, 2 * nbasis + 16), BF16),
            out_type((hidden, 2 * n_feat), F32),
            out_type((hidden, 2 * n_feat), BF16),
            out_type((n_feat, n_feat), BF16),
            out_type((8, n_feat), F32),
            out_type(w_o2.shape, BF16),
            out_type(w_o1.shape, BF16),
        ]
        + [out_type((1, n_feat), F32)] * 3
        + [out_type((tp, tile, tile), jnp.int32), pltpu.SMEM(tile_pairs.shape, jnp.int32)],
        [
            pltpu.VMEM(w_in.shape, BF16),
            pltpu.VMEM(w_f1.shape, BF16),
            pltpu.VMEM((1, hidden), F32),
            pltpu.VMEM(w_f2.shape, BF16),
            pltpu.VMEM((1, n_feat), F32),
            pltpu.SemaphoreType.DMA((12,)),
        ],
        60,
        w_in, w_f1, b_f1[None], w_f2, read_w[None], w_o2, w_o1, b_f2[None], b_o1[None], b_o2[None],
        masks[0, 0], tile_pairs,
    )
    col_pos = col_pos
    step = 1
    while step < n_col:
        col_pos = jnp.concatenate([col_pos, exchange(col_pos, "col", n_col, step)], axis=0)
        step *= 2

    def stack(held, got, *after):
        return run(
            stack_kernel, "stack_tiles", [VMEM, VMEM] + [ANY] * len(after),
            [out_type((2 * held.shape[0],) + held.shape[1:], BF16)], [], 4,
            held, got, *after,
        )[0]

    ready = [[w2], [col_pos]]
    own = near
    step = n_row // 2
    while step > 1:
        near = stack(near, exchange(near, "row", n_row, step), *(ready.pop(0) if ready else []))
        step //= 2
    far = exchange(near, "row", n_row, 1)
    count = pair_count

    plane = pltpu.VMEM((half, 2 * tile), F32)
    partial, partial16, tangents, proj, geom = run(
        pair_kernel, "pair_messages", [SMEM, SMEM] + [VMEM] * 8,
        [
            out_type((span, n_feat), F32),
            out_type((span, n_feat), BF16),
            out_type((tp, half, n_feat, 2 * tile), BF16),
            out_type((tp, n_feat, tile), BF16),
            out_type((tp, 5, half, 2 * tile), F32),
        ],
        [
            pltpu.VMEM((2 * tile, 2 * n_feat), BF16),
            plane, plane, plane, plane,
            pltpu.VMEM((CHUNK * hidden, 2 * tile), BF16),
        ],
        16,
        count, pairs, near, far, col_pos, masks, lhs, w2, w_in_t, b_f2,
    )

    step = 1
    while step < n_col // 2:
        partial = partial + exchange(partial16, "col", n_col, step).astype(F32)
        partial16 = partial.astype(BF16)
        step *= 2
    other = exchange(partial16, "col", n_col, step)

    features_out, keep, send, row_keep, row_send = run(
        force_kernel, "pair_forces",
        [SMEM, SMEM] + [VMEM] * 13,
        [
            pltpu.HBM((n_feat, owned), BF16),
            out_type((n_row // 2, 8, owned), F32),
            out_type((n_row // 2, 8, owned), F32),
            out_type((n_col // 2, 8, owned), F32),
            out_type((n_col // 2, 8, owned), F32),
        ],
        [
            pltpu.VMEM((n_feat, owned), BF16),
            pltpu.VMEM((span, n_feat), F32),
            pltpu.VMEM((span, n_feat), F32),
            pltpu.VMEM((2 * tile, 2 * n_feat), BF16),
            plane,
            pltpu.VMEM((CHUNK * hidden, 2 * n_feat), BF16),
            pltpu.VMEM((n_row, 8, owned), F32),
            pltpu.VMEM((n_col, 8, owned), F32),
            pltpu.SemaphoreType.DMA((1,)),
        ],
        16,
        count, pairs, partial, other, own, w_o1, b_o1, w_o2, b_o2, direction, w2_16, b_f2,
        proj, geom, tangents,
    )

    def reduce_halves(keep, send, axis, size):
        step = 1
        while True:
            other = exchange(send, axis, size, step)
            half = keep.shape[0] // 2
            step *= 2
            if step == size:
                return (keep + other)[0]
            send = keep[half:] + other[half:]
            keep = keep[:half] + other[:half]

    forces = reduce_halves(keep, send, "row", n_row) + reduce_halves(
        row_keep, row_send, "col", n_col
    )
    return (features_out, forces[:3])


def solution(mesh):
    atoms = P(None, ("row", "col"))
    in_specs = (
        atoms,
        atoms,
        P("row", "col", None, None),
        P("row", "col"),
        P("row", "col", None, None, None),
    ) + (P(),) * 10
    return jax.shard_map(
        local, mesh=mesh, in_specs=in_specs, out_specs=(atoms, atoms), check_vma=False
    )
```

```python
import math

import jax
import jax.numpy as jnp
from jax import lax
from jax.experimental import pallas as pl
from jax.experimental.pallas import tpu as pltpu
from jax.sharding import PartitionSpec as P

SOFTENING = 0.25
GAMMA_RBF = 10.0
CENTER_MAX = 10.0
CUTOFF = 12.0
LN2 = math.log(2.0)
SCALE = math.sqrt(GAMMA_RBF / LN2)
TANGENT = -GAMMA_RBF / SCALE
POS_ROWS = 16
MIB = 1024 * 1024
F32 = jnp.float32
BF16 = jnp.bfloat16


def dot(a, b):
    return jnp.dot(a, b, preferred_element_type=F32)


def dot_t(a, b):
    return lax.dot_general(a, b, (((1,), (1,)), ((), ())), preferred_element_type=F32)


def split2(x):
    hi = x.astype(BF16)
    return hi, (x - hi.astype(F32)).astype(BF16)


def fold(x):
    half = x.shape[0] // 2
    return jnp.concatenate([x[:half], x[half:]], axis=1)


def unfold(x):
    half = x.shape[1] // 2
    return jnp.concatenate([x[:, :half], x[:, half:]], axis=0)


def block_diag(x):
    zero = jnp.zeros_like(x)
    return jnp.concatenate(
        [jnp.concatenate([x, zero], axis=1), jnp.concatenate([zero, x], axis=1)], axis=0
    )


def reverse_bits(value, count):
    bits = count.bit_length() - 1
    out = jnp.int32(0)
    for k in range(bits):
        out = out | (((value >> k) & 1) << (bits - 1 - k))
    return out


def out_type(shape, dtype):
    return pltpu.VMEM(shape, dtype)


def spread(row, count):
    rows = jnp.broadcast_to(row, (16, row.shape[1])).astype(BF16)
    return jnp.concatenate([rows] * (count // 16), axis=0)


def sin_cos(angle):
    turn = angle - 0.5 * math.pi
    square = turn * turn
    odd, even = 0.0, 0.0
    for k in range(6, -1, -1):
        odd = odd * square + (-1.0) ** k / math.factorial(2 * k + 1)
        even = even * square + (-1.0) ** k / math.factorial(2 * k)
    return even, -(odd * turn)


def fetch(sources, targets, sems):
    copies = [
        pltpu.make_async_copy(src, dst, sems.at[k])
        for k, (src, dst) in enumerate(zip(sources, targets))
    ]
    for copy in copies:
        copy.start()
    for copy in copies:
        copy.wait()


def pack_kernel(features_hbm, positions_hbm, out, col_pos, features, positions, sems):
    fetch([features_hbm, positions_hbm], [features, positions], sems)
    n_feat = features.shape[0]
    col_pos[0] = jnp.concatenate([positions[...], jnp.zeros((5, positions.shape[1]), F32)], axis=0)
    out[0, :n_feat] = features[...]
    exact = positions[...]
    hi = exact.astype(BF16).astype(F32)
    mid = (exact - hi).astype(BF16).astype(F32)
    pad = jnp.zeros((POS_ROWS - 9, exact.shape[1]), F32)
    pieces = jnp.concatenate([hi, mid, exact - hi - mid, pad], axis=0)
    out[0, n_feat:] = pieces.astype(BF16)


def stack_kernel(held, got, *rest):
    out = rest[-1]
    out[: held.shape[0]] = held[...]
    out[held.shape[0] :] = got[...]


def weight_kernel(
    w_in_hbm, w_f1_hbm, b_f1_hbm, w_f2_hbm, read_w_hbm, w_o2_hbm, w_o1_hbm, b_f2_hbm, b_o1_hbm, b_o2_hbm, masks_hbm, pairs_hbm,
    lhs, w2, w2_16, w_in_t, direction, w_o2, w_o1, b_f2, b_o1, b_o2, masks, pairs,
    w_in, w_f1, b_f1, w_f2, read_w, sems,
):
    fetch(
        [
            w_in_hbm, w_f1_hbm, b_f1_hbm, w_f2_hbm, read_w_hbm, w_o2_hbm,
            w_o1_hbm, b_f2_hbm, b_o1_hbm, b_o2_hbm, masks_hbm, pairs_hbm,
        ],
        [w_in, w_f1, b_f1, w_f2, read_w, w_o2, w_o1, b_f2, b_o1, b_o2, masks, pairs],
        sems,
    )
    nbasis, hidden = w_f1.shape
    weights = w_f1[...].astype(F32)
    zero = jnp.zeros_like(weights)
    bias = b_f1[...] * 0.5
    b_hi = bias.astype(BF16).astype(F32)
    b_mid = (bias - b_hi).astype(BF16).astype(F32)
    b_lo = bias - b_hi - b_mid
    extra = jnp.concatenate([b_hi, b_mid, b_lo, jnp.zeros((13, hidden), F32)], axis=0)
    table = jnp.concatenate(
        [
            jnp.concatenate([0.5 * weights, zero], axis=1),
            jnp.concatenate([zero, weights], axis=1),
            jnp.concatenate([extra, jnp.zeros_like(extra)], axis=1),
            jnp.zeros((256 - 2 * nbasis - 16, 2 * hidden), F32),
        ],
        axis=0,
    )
    lhs[...] = table.T[:, : 2 * nbasis + 16].astype(BF16)
    wide = w_f2[...].astype(F32)
    w2[...] = jnp.concatenate([wide, wide], axis=1)
    w2_16[...] = w2[...].astype(BF16)
    w_in_t[...] = w_in[...].astype(F32).T.astype(BF16)
    readout = jnp.broadcast_to(read_w[...], (8, read_w.shape[1]))
    r_hi = readout.astype(BF16)
    r_mid, r_lo = split2(readout - r_hi.astype(F32))
    direction[...] = dot_t(r_hi, w_o2[...]) + (dot_t(r_mid, w_o2[...]) + dot_t(r_lo, w_o2[...]))


def pair_kernel(
    count, pairs, near, far, col_pos, masks, lhs, w2, w_in_t, b_f2,
    msg, msg16, tangents, proj_out, geom_out,
    diag, dist, coef_h, coef_x, rows, left,
):
    n_row = lax.axis_size("row")
    me_row = lax.axis_index("row")
    me_col = lax.axis_index("col")
    tile = masks.shape[2]
    hidden = w2.shape[0]
    nbasis = (lhs.shape[1] - 16) // 2
    msg[...] = jnp.zeros_like(msg)
    centers = lax.broadcasted_iota(jnp.int32, (nbasis, 2 * tile), 0).astype(F32) * (
        SCALE * CENTER_MAX / (nbasis - 1)
    )
    ones = jnp.ones((16, 2 * tile), BF16)

    @pl.loop(0, count[0, 0])
    def _(slot):
        row_tile, col_tile = pairs[0, 0, 0, slot], pairs[0, 0, 1, slot]
        place = reverse_bits(col_tile ^ me_row, n_row)
        half = n_row // 2
        index = place & (half - 1)
        block = jnp.where(place >= half, far[index], near[index])
        proj = dot(w_in_t[...], block[:tile]).astype(BF16)
        proj_out[slot] = proj
        proj_t = proj.astype(F32).T.astype(BF16)
        diag[...] = block_diag(proj_t)
        pieces = block[tile:].astype(F32)
        sender = pieces[0:3] + pieces[3:6] + pieces[6:9]
        receiver = col_pos[row_tile ^ me_col]
        square = jnp.zeros((tile, tile), F32)
        separation = []
        for k in range(3):
            up = jnp.broadcast_to(receiver[k : k + 1], (tile, tile)).T
            separation.append(up - sender[k : k + 1])
            square = square + separation[k] * separation[k]
        distance = jnp.sqrt(square + SOFTENING)
        angle = (math.pi / CUTOFF) * distance
        mask = masks[slot].astype(F32)
        sine, cosine = sin_cos(angle)
        cut = 0.5 * (cosine + 1.0) * mask
        dist[...] = fold(distance * SCALE)
        coef_h[...] = fold(-LN2 * cut)
        coef_x[...] = fold(sine / (cosine + 1.0) * (LN2 * math.pi / CUTOFF / TANGENT))
        inverse = 1.0 / distance
        for k in range(3):
            geom_out[slot, k] = fold(separation[k] * inverse)
        geom_out[slot, 3] = fold((-0.5 * math.pi / CUTOFF) * sine * mask)
        geom_out[slot, 4] = fold(cut * TANGENT)
        c_hi, c_lo = split2(cut)
        bias_part = (dot(c_hi, proj_t) + dot(c_lo, proj_t)) * b_f2[...]

        d, h, x = dist[...], coef_h[...], coef_x[...]
        for u in range(tile // 2):
            offset = d[u : u + 1] - centers
            gauss = jnp.exp2(-(offset * offset))
            basis = jnp.concatenate(
                [gauss.astype(BF16), (offset * gauss).astype(BF16), ones], axis=0
            )
            pre = dot(lhs[...], basis)
            bend = jnp.tanh(pre[:hidden])
            value = lax.log2(1.0 - bend)
            slope = (1.0 + bend) * pre[hidden:]
            value = value.astype(BF16)
            left[pl.ds(u * hidden, hidden), :] = spread(h[u : u + 1], hidden) * value
            tangents[slot, u] = spread(x[u : u + 1], hidden) * value + slope.astype(BF16)
        mixed = dot(left[...], diag[...])
        sums = [
            jnp.sum(mixed[u * hidden : (u + 1) * hidden] * w2[...], axis=0, keepdims=True)
            for u in range(tile // 2)
        ]
        rows[...] = jnp.concatenate(sums, axis=0)

        here = pl.ds(pl.multiple_of(row_tile * tile, tile), tile)
        msg[here, :] = msg[here, :] + (bias_part + unfold(rows[...]))

    msg16[...] = msg[...].astype(BF16)


def force_kernel(
    count, pairs, msg_a, msg_b, near, w_o1, b_o1, w_o2, b_o2, direction, w2_16, b_f2,
    proj, geom, tangents,
    features_hbm, keep, send, row_keep, row_send,
    features_out, grads, pre_act, diag, rows, left, force, row_force, sems,
):
    n_row = lax.axis_size("row")
    n_col = lax.axis_size("col")
    me_row = lax.axis_index("row")
    me_col = lax.axis_index("col")
    n_feat, tile = features_out.shape
    hidden = w2_16.shape[0]
    force[...] = jnp.zeros_like(force)
    row_force[...] = jnp.zeros_like(row_force)
    messages = (msg_a[...] + msg_b[...].astype(F32)).astype(BF16)
    pre = dot(messages, w_o1[...]) + b_o1[...]
    pre_act[...] = pre
    s_hi, s_lo = split2(direction[0:1] / (1.0 + jnp.exp(-pre)))
    grads[...] = dot_t(s_hi, w_o1[...]) + dot_t(s_lo, w_o1[...])
    own = pre_act[pl.ds(pl.multiple_of(me_col * tile, tile), tile), :]
    active = jnp.maximum(own, 0.0) + jnp.log(1.0 + jnp.exp(-jnp.abs(own))) - LN2
    update = dot(active.astype(BF16), w_o2[...]) + b_o2[...]
    features_out[...] = (near[0, :n_feat].astype(F32) + update.T).astype(BF16)
    store = pltpu.make_async_copy(features_out, features_hbm, sems.at[0])
    store.start()

    @pl.loop(0, count[0, 0])
    def _(slot):
        row_tile, col_tile = pairs[0, 0, 0, slot], pairs[0, 0, 1, slot]
        here = pl.ds(pl.multiple_of(row_tile * tile, tile), tile)
        grad_rows = grads[here, :]
        left_rows = fold(grad_rows)
        rows[...] = left_rows
        diag[...] = block_diag(proj[slot])

        g = rows[...]
        for u in range(tile // 2):
            left[pl.ds(u * hidden, hidden), :] = w2_16[...] * spread(g[u : u + 1], hidden)
        mixed = dot(left[...], diag[...])
        sums = [
            jnp.sum(
                mixed[u * hidden : (u + 1) * hidden] * tangents[slot, u].astype(F32),
                axis=0,
                keepdims=True,
            )
            for u in range(tile // 2)
        ]
        rows[...] = jnp.concatenate(sums, axis=0)

        g_hi, g_lo = split2(grad_rows * b_f2[...])
        bias_part = dot(g_hi, proj[slot]) + dot(g_lo, proj[slot])
        dist_grad = unfold(geom[slot, 4] * rows[...]) + unfold(geom[slot, 3]) * bias_part
        to_rows, to_cols = [], []
        for k in range(3):
            push = unfold(geom[slot, k]) * dist_grad
            to_cols.append(jnp.sum(push, axis=0, keepdims=True))
            to_rows.append(-jnp.sum(push.T, axis=0, keepdims=True))
        zero = jnp.zeros((5, tile), F32)
        place = reverse_bits(col_tile ^ me_row, n_row)
        force[place] = force[place] + jnp.concatenate(to_cols + [zero], axis=0)
        place = reverse_bits(row_tile ^ me_col, n_col)
        row_force[place] = row_force[place] + jnp.concatenate(to_rows + [zero], axis=0)

    keep[...] = force[: n_row // 2]
    send[...] = force[n_row // 2 :]
    row_keep[...] = row_force[: n_col // 2]
    row_send[...] = row_force[n_col // 2 :]
    store.wait()


def exchange(value, axis, size, step):
    return lax.ppermute(value, axis, [(i, i ^ step) for i in range(size)])


ANY = pl.BlockSpec(memory_space=pl.ANY)
SMEM = pl.BlockSpec(memory_space=pltpu.SMEM)
VMEM = pl.BlockSpec(memory_space=pltpu.VMEM)
HBM = pl.BlockSpec(memory_space=pltpu.HBM)


def run(kernel, name, specs, out_shape, scratch, limit, *operands):
    return pl.pallas_call(
        kernel,
        in_specs=specs,
        out_specs=[pl.BlockSpec(memory_space=x.memory_space) for x in out_shape],
        out_shape=out_shape,
        scratch_shapes=scratch,
        compiler_params=pltpu.CompilerParams(vmem_limit_bytes=limit * MIB),
        name=name,
    )(*operands)


def local(
    features, positions, tile_pairs, pair_count, masks,
    w_in, w_f1, b_f1, w_f2, b_f2, w_o1, b_o1, w_o2, b_o2, read_w,
):
    n_feat, owned = features.shape
    tile = masks.shape[-1]
    tp = masks.shape[2]
    n_row = lax.axis_size("row")
    n_col = lax.axis_size("col")
    span = n_col * owned
    half = tile // 2
    nbasis, hidden = w_f1.shape

    near, col_pos = run(
        pack_kernel, "pack_tile", [HBM, HBM],
        [out_type((1, n_feat + POS_ROWS, owned), BF16), out_type((1, 8, owned), F32)],
        [
            pltpu.VMEM(features.shape, BF16),
            pltpu.VMEM(positions.shape, F32),
            pltpu.SemaphoreType.DMA((2,)),
        ],
        60,
        features, positions,
    )
    lhs, w2, w2_16, w_in_t, direction, w_o2, w_o1, b_f2, b_o1, b_o2, masks, pairs = run(
        weight_kernel, "weight_tables", [HBM] * 12,
        [
            out_type((2 * hidden, 2 * nbasis + 16), BF16),
            out_type((hidden, 2 * n_feat), F32),
            out_type((hidden, 2 * n_feat), BF16),
            out_type((n_feat, n_feat), BF16),
            out_type((8, n_feat), F32),
            out_type(w_o2.shape, BF16),
            out_type(w_o1.shape, BF16),
        ]
        + [out_type((1, n_feat), F32)] * 3
        + [out_type((tp, tile, tile), jnp.int32), pltpu.SMEM(tile_pairs.shape, jnp.int32)],
        [
            pltpu.VMEM(w_in.shape, BF16),
            pltpu.VMEM(w_f1.shape, BF16),
            pltpu.VMEM((1, hidden), F32),
            pltpu.VMEM(w_f2.shape, BF16),
            pltpu.VMEM((1, n_feat), F32),
            pltpu.SemaphoreType.DMA((12,)),
        ],
        60,
        w_in, w_f1, b_f1[None], w_f2, read_w[None], w_o2, w_o1, b_f2[None], b_o1[None], b_o2[None],
        masks[0, 0], tile_pairs,
    )
    col_pos = col_pos
    step = 1
    while step < n_col:
        col_pos = jnp.concatenate([col_pos, exchange(col_pos, "col", n_col, step)], axis=0)
        step *= 2

    def stack(held, got, *after):
        return run(
            stack_kernel, "stack_tiles", [VMEM, VMEM] + [ANY] * len(after),
            [out_type((2 * held.shape[0],) + held.shape[1:], BF16)], [], 4,
            held, got, *after,
        )[0]

    ready = [[w2], [col_pos]]
    own = near
    step = n_row // 2
    while step > 1:
        near = stack(near, exchange(near, "row", n_row, step), *(ready.pop(0) if ready else []))
        step //= 2
    far = exchange(near, "row", n_row, 1)
    count = pair_count

    plane = pltpu.VMEM((half, 2 * tile), F32)
    partial, partial16, tangents, proj, geom = run(
        pair_kernel, "pair_messages", [SMEM, SMEM] + [VMEM] * 8,
        [
            out_type((span, n_feat), F32),
            out_type((span, n_feat), BF16),
            out_type((tp, half, n_feat, 2 * tile), BF16),
            out_type((tp, n_feat, tile), BF16),
            out_type((tp, 5, half, 2 * tile), F32),
        ],
        [
            pltpu.VMEM((2 * tile, 2 * n_feat), BF16),
            plane, plane, plane, plane,
            pltpu.VMEM((half * hidden, 2 * tile), BF16),
        ],
        16,
        count, pairs, near, far, col_pos, masks, lhs, w2, w_in_t, b_f2,
    )

    step = 1
    while step < n_col // 2:
        partial = partial + exchange(partial16, "col", n_col, step).astype(F32)
        partial16 = partial.astype(BF16)
        step *= 2
    other = exchange(partial16, "col", n_col, step)

    features_out, keep, send, row_keep, row_send = run(
        force_kernel, "pair_forces",
        [SMEM, SMEM] + [VMEM] * 13,
        [
            pltpu.HBM((n_feat, owned), BF16),
            out_type((n_row // 2, 8, owned), F32),
            out_type((n_row // 2, 8, owned), F32),
            out_type((n_col // 2, 8, owned), F32),
            out_type((n_col // 2, 8, owned), F32),
        ],
        [
            pltpu.VMEM((n_feat, owned), BF16),
            pltpu.VMEM((span, n_feat), F32),
            pltpu.VMEM((span, n_feat), F32),
            pltpu.VMEM((2 * tile, 2 * n_feat), BF16),
            plane,
            pltpu.VMEM((half * hidden, 2 * n_feat), BF16),
            pltpu.VMEM((n_row, 8, owned), F32),
            pltpu.VMEM((n_col, 8, owned), F32),
            pltpu.SemaphoreType.DMA((1,)),
        ],
        16,
        count, pairs, partial, other, own, w_o1, b_o1, w_o2, b_o2, direction, w2_16, b_f2,
        proj, geom, tangents,
    )

    def reduce_halves(keep, send, axis, size):
        step = 1
        while True:
            other = exchange(send, axis, size, step)
            half = keep.shape[0] // 2
            step *= 2
            if step == size:
                return (keep + other)[0]
            send = keep[half:] + other[half:]
            keep = keep[:half] + other[:half]

    forces = reduce_halves(keep, send, "row", n_row) + reduce_halves(
        row_keep, row_send, "col", n_col
    )
    return (features_out, forces[:3])


def solution(mesh):
    atoms = P(None, ("row", "col"))
    in_specs = (
        atoms,
        atoms,
        P("row", "col", None, None),
        P("row", "col"),
        P("row", "col", None, None, None),
    ) + (P(),) * 10
    return jax.shard_map(
        local, mesh=mesh, in_specs=in_specs, out_specs=(atoms, atoms), check_vma=False
    )
```

```python
import math

import jax
import jax.numpy as jnp
from jax import lax
from jax.experimental import pallas as pl
from jax.experimental.pallas import tpu as pltpu
from jax.sharding import PartitionSpec as P

SOFTENING = 0.25
GAMMA_RBF = 10.0
CENTER_MAX = 10.0
CUTOFF = 12.0
LN2 = math.log(2.0)
SCALE = math.sqrt(GAMMA_RBF / LN2)
TANGENT = -GAMMA_RBF / SCALE
POS_ROWS = 16
MIB = 1024 * 1024
F32 = jnp.float32
BF16 = jnp.bfloat16


def dot(a, b):
    return jnp.dot(a, b, preferred_element_type=F32)


def dot_t(a, b):
    return lax.dot_general(a, b, (((1,), (1,)), ((), ())), preferred_element_type=F32)


def split2(x):
    hi = x.astype(BF16)
    return hi, (x - hi.astype(F32)).astype(BF16)


def fold(x):
    half = x.shape[0] // 2
    return jnp.concatenate([x[:half], x[half:]], axis=1)


def unfold(x):
    half = x.shape[1] // 2
    return jnp.concatenate([x[:, :half], x[:, half:]], axis=0)


def block_diag(x):
    zero = jnp.zeros_like(x)
    return jnp.concatenate(
        [jnp.concatenate([x, zero], axis=1), jnp.concatenate([zero, x], axis=1)], axis=0
    )


def reverse_bits(value, count):
    bits = count.bit_length() - 1
    out = jnp.int32(0)
    for k in range(bits):
        out = out | (((value >> k) & 1) << (bits - 1 - k))
    return out


def out_type(shape, dtype):
    return pltpu.VMEM(shape, dtype)


def spread(row, count):
    rows = jnp.broadcast_to(row, (16, row.shape[1])).astype(BF16)
    return jnp.concatenate([rows] * (count // 16), axis=0)


def sin_cos(angle):
    turn = angle - 0.5 * math.pi
    square = turn * turn
    odd, even = 0.0, 0.0
    for k in range(6, -1, -1):
        odd = odd * square + (-1.0) ** k / math.factorial(2 * k + 1)
        even = even * square + (-1.0) ** k / math.factorial(2 * k)
    return even, -(odd * turn)


def fetch(sources, targets, sems):
    copies = [
        pltpu.make_async_copy(src, dst, sems.at[k])
        for k, (src, dst) in enumerate(zip(sources, targets))
    ]
    for copy in copies:
        copy.start()
    for copy in copies:
        copy.wait()


def pack_kernel(features_hbm, positions_hbm, out, col_pos, features, positions, sems):
    fetch([features_hbm, positions_hbm], [features, positions], sems)
    n_feat = features.shape[0]
    col_pos[0] = jnp.concatenate([positions[...], jnp.zeros((5, positions.shape[1]), F32)], axis=0)
    out[0, :n_feat] = features[...]
    exact = positions[...]
    hi = exact.astype(BF16).astype(F32)
    mid = (exact - hi).astype(BF16).astype(F32)
    pad = jnp.zeros((POS_ROWS - 9, exact.shape[1]), F32)
    pieces = jnp.concatenate([hi, mid, exact - hi - mid, pad], axis=0)
    out[0, n_feat:] = pieces.astype(BF16)


def stack_kernel(held, got, *rest):
    out = rest[-1]
    out[: held.shape[0]] = held[...]
    out[held.shape[0] :] = got[...]


def weight_kernel(
    w_in_hbm, w_f1_hbm, b_f1_hbm, w_f2_hbm, read_w_hbm, w_o2_hbm, w_o1_hbm, b_f2_hbm, b_o1_hbm, b_o2_hbm, masks_hbm, pairs_hbm,
    lhs, lhs_t, w2, w2_16, w_in_t, direction, w_o2, w_o1, b_f2, b_o1, b_o2, masks, pairs,
    w_in, w_f1, b_f1, w_f2, read_w, sems,
):
    fetch(
        [
            w_in_hbm, w_f1_hbm, b_f1_hbm, w_f2_hbm, read_w_hbm, w_o2_hbm,
            w_o1_hbm, b_f2_hbm, b_o1_hbm, b_o2_hbm, masks_hbm, pairs_hbm,
        ],
        [w_in, w_f1, b_f1, w_f2, read_w, w_o2, w_o1, b_f2, b_o1, b_o2, masks, pairs],
        sems,
    )
    nbasis, hidden = w_f1.shape
    weights = w_f1[...].astype(F32)
    bias = b_f1[...] * 0.5
    b_hi = bias.astype(BF16).astype(F32)
    b_mid = (bias - b_hi).astype(BF16).astype(F32)
    b_lo = bias - b_hi - b_mid
    extra = jnp.concatenate([b_hi, b_mid, b_lo, jnp.zeros((13, hidden), F32)], axis=0)
    table = jnp.concatenate(
        [
            jnp.concatenate([0.5 * weights, weights], axis=1),
            jnp.concatenate([extra, jnp.zeros_like(extra)], axis=1),
            jnp.zeros((128 - nbasis - 16, 2 * hidden), F32),
        ],
        axis=0,
    )
    flipped = table.T.astype(BF16)
    lhs[...] = flipped[:hidden, : nbasis + 16]
    lhs_t[...] = flipped[hidden:, :nbasis]
    wide = w_f2[...].astype(F32)
    w2[...] = jnp.concatenate([wide, wide], axis=1)
    w2_16[...] = w2[...].astype(BF16)
    w_in_t[...] = w_in[...].astype(F32).T.astype(BF16)
    readout = jnp.broadcast_to(read_w[...], (8, read_w.shape[1]))
    r_hi = readout.astype(BF16)
    r_mid, r_lo = split2(readout - r_hi.astype(F32))
    direction[...] = dot_t(r_hi, w_o2[...]) + (dot_t(r_mid, w_o2[...]) + dot_t(r_lo, w_o2[...]))


def pair_kernel(
    count, pairs, near, far, col_pos, masks, lhs, lhs_t, w2, w_in_t, b_f2,
    msg, msg16, tangents, proj_out, geom_out,
    diag, dist, coef_h, coef_x, rows, left,
):
    n_row = lax.axis_size("row")
    me_row = lax.axis_index("row")
    me_col = lax.axis_index("col")
    tile = masks.shape[2]
    hidden = w2.shape[0]
    nbasis = lhs.shape[1] - 16
    msg[...] = jnp.zeros_like(msg)
    centers = lax.broadcasted_iota(jnp.int32, (nbasis, 2 * tile), 0).astype(F32) * (
        SCALE * CENTER_MAX / (nbasis - 1)
    )
    ones = jnp.ones((16, 2 * tile), BF16)

    @pl.loop(0, count[0, 0])
    def _(slot):
        row_tile, col_tile = pairs[0, 0, 0, slot], pairs[0, 0, 1, slot]
        place = reverse_bits(col_tile ^ me_row, n_row)
        half = n_row // 2
        index = place & (half - 1)
        block = jnp.where(place >= half, far[index], near[index])
        proj = dot(w_in_t[...], block[:tile]).astype(BF16)
        proj_out[slot] = proj
        proj_t = proj.astype(F32).T.astype(BF16)
        diag[...] = block_diag(proj_t)
        pieces = block[tile:].astype(F32)
        sender = pieces[0:3] + pieces[3:6] + pieces[6:9]
        receiver = col_pos[row_tile ^ me_col]
        square = jnp.zeros((tile, tile), F32)
        separation = []
        for k in range(3):
            up = jnp.broadcast_to(receiver[k : k + 1], (tile, tile)).T
            separation.append(up - sender[k : k + 1])
            square = square + separation[k] * separation[k]
        distance = jnp.sqrt(square + SOFTENING)
        angle = (math.pi / CUTOFF) * distance
        mask = masks[slot].astype(F32)
        sine, cosine = sin_cos(angle)
        cut = 0.5 * (cosine + 1.0) * mask
        dist[...] = fold(distance * SCALE)
        coef_h[...] = fold(-LN2 * cut)
        coef_x[...] = fold(sine / (cosine + 1.0) * (LN2 * math.pi / CUTOFF / TANGENT))
        inverse = 1.0 / distance
        for k in range(3):
            geom_out[slot, k] = fold(separation[k] * inverse)
        geom_out[slot, 3] = fold((-0.5 * math.pi / CUTOFF) * sine * mask)
        geom_out[slot, 4] = fold(cut * TANGENT)
        c_hi, c_lo = split2(cut)
        bias_part = (dot(c_hi, proj_t) + dot(c_lo, proj_t)) * b_f2[...]

        d, h, x = dist[...], coef_h[...], coef_x[...]
        for u in range(tile // 2):
            offset = d[u : u + 1] - centers
            gauss = jnp.exp2(-(offset * offset))
            gauss = gauss.astype(BF16)
            basis = jnp.concatenate([gauss, ones], axis=0)
            bend = jnp.tanh(dot(lhs[...], basis))
            value = lax.log2(1.0 - bend).astype(BF16)
            along = dot(lhs_t[...], offset.astype(BF16) * gauss).astype(BF16)
            slope = (1.0 + bend).astype(BF16) * along
            left[pl.ds(u * hidden, hidden), :] = spread(h[u : u + 1], hidden) * value
            tangents[slot, u] = spread(x[u : u + 1], hidden) * value + slope
        mixed = dot(left[...], diag[...])
        sums = [
            jnp.sum(mixed[u * hidden : (u + 1) * hidden] * w2[...], axis=0, keepdims=True)
            for u in range(tile // 2)
        ]
        rows[...] = jnp.concatenate(sums, axis=0)

        here = pl.ds(pl.multiple_of(row_tile * tile, tile), tile)
        msg[here, :] = msg[here, :] + (bias_part + unfold(rows[...]))

    msg16[...] = msg[...].astype(BF16)


def force_kernel(
    count, pairs, msg_a, msg_b, near, w_o1, b_o1, w_o2, b_o2, direction, w2_16, b_f2,
    proj, geom, tangents,
    features_hbm, keep, send, row_keep, row_send,
    features_out, grads, pre_act, diag, rows, left, force, row_force, sems,
):
    n_row = lax.axis_size("row")
    n_col = lax.axis_size("col")
    me_row = lax.axis_index("row")
    me_col = lax.axis_index("col")
    n_feat, tile = features_out.shape
    hidden = w2_16.shape[0]
    force[...] = jnp.zeros_like(force)
    row_force[...] = jnp.zeros_like(row_force)
    messages = (msg_a[...] + msg_b[...].astype(F32)).astype(BF16)
    pre = dot(messages, w_o1[...]) + b_o1[...]
    pre_act[...] = pre
    s_hi, s_lo = split2(direction[0:1] / (1.0 + jnp.exp(-pre)))
    grads[...] = dot_t(s_hi, w_o1[...]) + dot_t(s_lo, w_o1[...])
    own = pre_act[pl.ds(pl.multiple_of(me_col * tile, tile), tile), :]
    active = jnp.maximum(own, 0.0) + jnp.log(1.0 + jnp.exp(-jnp.abs(own))) - LN2
    update = dot(active.astype(BF16), w_o2[...]) + b_o2[...]
    features_out[...] = (near[0, :n_feat].astype(F32) + update.T).astype(BF16)
    store = pltpu.make_async_copy(features_out, features_hbm, sems.at[0])
    store.start()

    @pl.loop(0, count[0, 0])
    def _(slot):
        row_tile, col_tile = pairs[0, 0, 0, slot], pairs[0, 0, 1, slot]
        here = pl.ds(pl.multiple_of(row_tile * tile, tile), tile)
        grad_rows = grads[here, :]
        left_rows = fold(grad_rows)
        rows[...] = left_rows
        diag[...] = block_diag(proj[slot])

        g = rows[...]
        for u in range(tile // 2):
            left[pl.ds(u * hidden, hidden), :] = w2_16[...] * spread(g[u : u + 1], hidden)
        mixed = dot(left[...], diag[...])
        sums = [
            jnp.sum(
                mixed[u * hidden : (u + 1) * hidden] * tangents[slot, u].astype(F32),
                axis=0,
                keepdims=True,
            )
            for u in range(tile // 2)
        ]
        rows[...] = jnp.concatenate(sums, axis=0)

        g_hi, g_lo = split2(grad_rows * b_f2[...])
        bias_part = dot(g_hi, proj[slot]) + dot(g_lo, proj[slot])
        dist_grad = unfold(geom[slot, 4] * rows[...]) + unfold(geom[slot, 3]) * bias_part
        to_rows, to_cols = [], []
        for k in range(3):
            push = unfold(geom[slot, k]) * dist_grad
            to_cols.append(jnp.sum(push, axis=0, keepdims=True))
            to_rows.append(-jnp.sum(push.T, axis=0, keepdims=True))
        zero = jnp.zeros((5, tile), F32)
        place = reverse_bits(col_tile ^ me_row, n_row)
        force[place] = force[place] + jnp.concatenate(to_cols + [zero], axis=0)
        place = reverse_bits(row_tile ^ me_col, n_col)
        row_force[place] = row_force[place] + jnp.concatenate(to_rows + [zero], axis=0)

    keep[...] = force[: n_row // 2]
    send[...] = force[n_row // 2 :]
    row_keep[...] = row_force[: n_col // 2]
    row_send[...] = row_force[n_col // 2 :]
    store.wait()


def exchange(value, axis, size, step):
    return lax.ppermute(value, axis, [(i, i ^ step) for i in range(size)])


ANY = pl.BlockSpec(memory_space=pl.ANY)
SMEM = pl.BlockSpec(memory_space=pltpu.SMEM)
VMEM = pl.BlockSpec(memory_space=pltpu.VMEM)
HBM = pl.BlockSpec(memory_space=pltpu.HBM)


def run(kernel, name, specs, out_shape, scratch, limit, *operands):
    return pl.pallas_call(
        kernel,
        in_specs=specs,
        out_specs=[pl.BlockSpec(memory_space=x.memory_space) for x in out_shape],
        out_shape=out_shape,
        scratch_shapes=scratch,
        compiler_params=pltpu.CompilerParams(vmem_limit_bytes=limit * MIB),
        name=name,
    )(*operands)


def local(
    features, positions, tile_pairs, pair_count, masks,
    w_in, w_f1, b_f1, w_f2, b_f2, w_o1, b_o1, w_o2, b_o2, read_w,
):
    n_feat, owned = features.shape
    tile = masks.shape[-1]
    tp = masks.shape[2]
    n_row = lax.axis_size("row")
    n_col = lax.axis_size("col")
    span = n_col * owned
    half = tile // 2
    nbasis, hidden = w_f1.shape

    near, col_pos = run(
        pack_kernel, "pack_tile", [HBM, HBM],
        [out_type((1, n_feat + POS_ROWS, owned), BF16), out_type((1, 8, owned), F32)],
        [
            pltpu.VMEM(features.shape, BF16),
            pltpu.VMEM(positions.shape, F32),
            pltpu.SemaphoreType.DMA((2,)),
        ],
        60,
        features, positions,
    )
    lhs, lhs_t, w2, w2_16, w_in_t, direction, w_o2, w_o1, b_f2, b_o1, b_o2, masks, pairs = run(
        weight_kernel, "weight_tables", [HBM] * 12,
        [
            out_type((hidden, nbasis + 16), BF16),
            out_type((hidden, nbasis), BF16),
            out_type((hidden, 2 * n_feat), F32),
            out_type((hidden, 2 * n_feat), BF16),
            out_type((n_feat, n_feat), BF16),
            out_type((8, n_feat), F32),
            out_type(w_o2.shape, BF16),
            out_type(w_o1.shape, BF16),
        ]
        + [out_type((1, n_feat), F32)] * 3
        + [out_type((tp, tile, tile), jnp.int32), pltpu.SMEM(tile_pairs.shape, jnp.int32)],
        [
            pltpu.VMEM(w_in.shape, BF16),
            pltpu.VMEM(w_f1.shape, BF16),
            pltpu.VMEM((1, hidden), F32),
            pltpu.VMEM(w_f2.shape, BF16),
            pltpu.VMEM((1, n_feat), F32),
            pltpu.SemaphoreType.DMA((12,)),
        ],
        60,
        w_in, w_f1, b_f1[None], w_f2, read_w[None], w_o2, w_o1, b_f2[None], b_o1[None], b_o2[None],
        masks[0, 0], tile_pairs,
    )
    col_pos = col_pos
    step = 1
    while step < n_col:
        col_pos = jnp.concatenate([col_pos, exchange(col_pos, "col", n_col, step)], axis=0)
        step *= 2

    def stack(held, got, *after):
        return run(
            stack_kernel, "stack_tiles", [VMEM, VMEM] + [ANY] * len(after),
            [out_type((2 * held.shape[0],) + held.shape[1:], BF16)], [], 4,
            held, got, *after,
        )[0]

    ready = [[w2], [col_pos]]
    own = near
    step = n_row // 2
    while step > 1:
        near = stack(near, exchange(near, "row", n_row, step), *(ready.pop(0) if ready else []))
        step //= 2
    far = exchange(near, "row", n_row, 1)
    count = pair_count

    plane = pltpu.VMEM((half, 2 * tile), F32)
    partial, partial16, tangents, proj, geom = run(
        pair_kernel, "pair_messages", [SMEM, SMEM] + [VMEM] * 9,
        [
            out_type((span, n_feat), F32),
            out_type((span, n_feat), BF16),
            out_type((tp, half, n_feat, 2 * tile), BF16),
            out_type((tp, n_feat, tile), BF16),
            out_type((tp, 5, half, 2 * tile), F32),
        ],
        [
            pltpu.VMEM((2 * tile, 2 * n_feat), BF16),
            plane, plane, plane, plane,
            pltpu.VMEM((half * hidden, 2 * tile), BF16),
        ],
        16,
        count, pairs, near, far, col_pos, masks, lhs, lhs_t, w2, w_in_t, b_f2,
    )

    step = 1
    while step < n_col // 2:
        partial = partial + exchange(partial16, "col", n_col, step).astype(F32)
        partial16 = partial.astype(BF16)
        step *= 2
    other = exchange(partial16, "col", n_col, step)

    features_out, keep, send, row_keep, row_send = run(
        force_kernel, "pair_forces",
        [SMEM, SMEM] + [VMEM] * 13,
        [
            pltpu.HBM((n_feat, owned), BF16),
            out_type((n_row // 2, 8, owned), F32),
            out_type((n_row // 2, 8, owned), F32),
            out_type((n_col // 2, 8, owned), F32),
            out_type((n_col // 2, 8, owned), F32),
        ],
        [
            pltpu.VMEM((n_feat, owned), BF16),
            pltpu.VMEM((span, n_feat), F32),
            pltpu.VMEM((span, n_feat), F32),
            pltpu.VMEM((2 * tile, 2 * n_feat), BF16),
            plane,
            pltpu.VMEM((half * hidden, 2 * n_feat), BF16),
            pltpu.VMEM((n_row, 8, owned), F32),
            pltpu.VMEM((n_col, 8, owned), F32),
            pltpu.SemaphoreType.DMA((1,)),
        ],
        16,
        count, pairs, partial, other, own, w_o1, b_o1, w_o2, b_o2, direction, w2_16, b_f2,
        proj, geom, tangents,
    )

    def reduce_halves(keep, send, axis, size):
        step = 1
        while True:
            other = exchange(send, axis, size, step)
            half = keep.shape[0] // 2
            step *= 2
            if step == size:
                return (keep + other)[0]
            send = keep[half:] + other[half:]
            keep = keep[:half] + other[:half]

    forces = reduce_halves(keep, send, "row", n_row) + reduce_halves(
        row_keep, row_send, "col", n_col
    )
    return (features_out, forces[:3])


def solution(mesh):
    atoms = P(None, ("row", "col"))
    in_specs = (
        atoms,
        atoms,
        P("row", "col", None, None),
        P("row", "col"),
        P("row", "col", None, None, None),
    ) + (P(),) * 10
    return jax.shard_map(
        local, mesh=mesh, in_specs=in_specs, out_specs=(atoms, atoms), check_vma=False
    )
```

```python
import math

import jax
import jax.numpy as jnp
from jax import lax
from jax.experimental import pallas as pl
from jax.experimental.pallas import tpu as pltpu
from jax.sharding import PartitionSpec as P

SOFTENING = 0.25
GAMMA_RBF = 10.0
CENTER_MAX = 10.0
CUTOFF = 12.0
LN2 = math.log(2.0)
SCALE = math.sqrt(GAMMA_RBF / LN2)
TANGENT = -GAMMA_RBF / SCALE
POS_ROWS = 16
MIB = 1024 * 1024
F32 = jnp.float32
BF16 = jnp.bfloat16


def dot(a, b):
    return jnp.dot(a, b, preferred_element_type=F32)


def dot_t(a, b):
    return lax.dot_general(a, b, (((1,), (1,)), ((), ())), preferred_element_type=F32)


def split2(x):
    hi = x.astype(BF16)
    return hi, (x - hi.astype(F32)).astype(BF16)


def fold(x):
    half = x.shape[0] // 2
    return jnp.concatenate([x[:half], x[half:]], axis=1)


def unfold(x):
    half = x.shape[1] // 2
    return jnp.concatenate([x[:, :half], x[:, half:]], axis=0)


def block_diag(x):
    zero = jnp.zeros_like(x)
    return jnp.concatenate(
        [jnp.concatenate([x, zero], axis=1), jnp.concatenate([zero, x], axis=1)], axis=0
    )


def reverse_bits(value, count):
    bits = count.bit_length() - 1
    out = jnp.int32(0)
    for k in range(bits):
        out = out | (((value >> k) & 1) << (bits - 1 - k))
    return out


def out_type(shape, dtype):
    return pltpu.VMEM(shape, dtype)


def stage_orders(n_row):
    steps = [n_row >> k for k in range(1, n_row.bit_length() - 1)]
    return steps, steps[-1:] + steps[:-1]


def stage_bits(value, steps):
    out = jnp.int32(0)
    for k, step in enumerate(steps):
        out = out | (((value >> (step.bit_length() - 1)) & 1) << k)
    return out


def spread(row, count):
    rows = jnp.broadcast_to(row, (16, row.shape[1])).astype(BF16)
    return jnp.concatenate([rows] * (count // 16), axis=0)


def sin_cos(angle):
    turn = angle - 0.5 * math.pi
    square = turn * turn
    odd, even = 0.0, 0.0
    for k in range(6, -1, -1):
        odd = odd * square + (-1.0) ** k / math.factorial(2 * k + 1)
        even = even * square + (-1.0) ** k / math.factorial(2 * k)
    return even, -(odd * turn)


def fetch(sources, targets, sems):
    copies = [
        pltpu.make_async_copy(src, dst, sems.at[k])
        for k, (src, dst) in enumerate(zip(sources, targets))
    ]
    for copy in copies:
        copy.start()
    for copy in copies:
        copy.wait()


def pack_kernel(features_hbm, positions_hbm, out, col_pos, features, positions, sems):
    fetch([features_hbm, positions_hbm], [features, positions], sems)
    n_feat = features.shape[0]
    col_pos[0] = jnp.concatenate([positions[...], jnp.zeros((5, positions.shape[1]), F32)], axis=0)
    out[0, :n_feat] = features[...]
    exact = positions[...]
    hi = exact.astype(BF16).astype(F32)
    mid = (exact - hi).astype(BF16).astype(F32)
    pad = jnp.zeros((POS_ROWS - 9, exact.shape[1]), F32)
    pieces = jnp.concatenate([hi, mid, exact - hi - mid, pad], axis=0)
    out[0, n_feat:] = pieces.astype(BF16)


def stack_kernel(held, got, *rest):
    out = rest[-1]
    out[: held.shape[0]] = held[...]
    out[held.shape[0] :] = got[...]


def weight_kernel(
    w_in_hbm, w_f1_hbm, b_f1_hbm, w_f2_hbm, read_w_hbm, w_o2_hbm, w_o1_hbm, b_f2_hbm, b_o1_hbm, b_o2_hbm, masks_hbm, pairs_hbm,
    lhs, lhs_t, w2, w2_16, w_in_t, direction, w_o2, w_o1, b_f2, b_o1, b_o2, masks, pairs,
    w_in, w_f1, b_f1, w_f2, read_w, sems,
):
    fetch(
        [
            w_in_hbm, w_f1_hbm, b_f1_hbm, w_f2_hbm, read_w_hbm, w_o2_hbm,
            w_o1_hbm, b_f2_hbm, b_o1_hbm, b_o2_hbm, masks_hbm, pairs_hbm,
        ],
        [w_in, w_f1, b_f1, w_f2, read_w, w_o2, w_o1, b_f2, b_o1, b_o2, masks, pairs],
        sems,
    )
    nbasis, hidden = w_f1.shape
    weights = w_f1[...].astype(F32)
    bias = b_f1[...] * 0.5
    b_hi = bias.astype(BF16).astype(F32)
    b_mid = (bias - b_hi).astype(BF16).astype(F32)
    b_lo = bias - b_hi - b_mid
    extra = jnp.concatenate([b_hi, b_mid, b_lo, jnp.zeros((13, hidden), F32)], axis=0)
    table = jnp.concatenate(
        [
            jnp.concatenate([0.5 * weights, weights], axis=1),
            jnp.concatenate([extra, jnp.zeros_like(extra)], axis=1),
            jnp.zeros((128 - nbasis - 16, 2 * hidden), F32),
        ],
        axis=0,
    )
    flipped = table.T.astype(BF16)
    lhs[...] = flipped[:hidden, : nbasis + 16]
    lhs_t[...] = flipped[hidden:, :nbasis]
    wide = w_f2[...].astype(F32)
    w2[...] = jnp.concatenate([wide, wide], axis=1)
    w2_16[...] = w2[...].astype(BF16)
    w_in_t[...] = w_in[...].astype(F32).T.astype(BF16)
    readout = jnp.broadcast_to(read_w[...], (8, read_w.shape[1]))
    r_hi = readout.astype(BF16)
    r_mid, r_lo = split2(readout - r_hi.astype(F32))
    direction[...] = dot_t(r_hi, w_o2[...]) + (dot_t(r_mid, w_o2[...]) + dot_t(r_lo, w_o2[...]))


def pair_kernel(
    count, pairs, near, far, col_pos, masks, lhs, lhs_t, w2, w_in_t, b_f2,
    msg, msg16, tangents, proj_out, geom_out,
    diag, dist, coef_h, coef_x, rows, left,
):
    n_row = lax.axis_size("row")
    me_row = lax.axis_index("row")
    me_col = lax.axis_index("col")
    tile = masks.shape[2]
    hidden = w2.shape[0]
    nbasis = lhs.shape[1] - 16
    msg[...] = jnp.zeros_like(msg)
    centers = lax.broadcasted_iota(jnp.int32, (nbasis, 2 * tile), 0).astype(F32) * (
        SCALE * CENTER_MAX / (nbasis - 1)
    )
    ones = jnp.ones((16, 2 * tile), BF16)

    @pl.loop(0, count[0, 0])
    def _(slot):
        row_tile, col_tile = pairs[0, 0, 0, slot], pairs[0, 0, 1, slot]
        apart = col_tile ^ me_row
        even, odd = (stage_bits(apart, order) for order in stage_orders(n_row))
        is_odd = (me_row & 1) == 1
        mine, other = jnp.where(is_odd, odd, even), jnp.where(is_odd, even, odd)
        block = jnp.where((apart & 1) == 1, far[other], near[mine])
        proj = dot(w_in_t[...], block[:tile]).astype(BF16)
        proj_out[slot] = proj
        proj_t = proj.astype(F32).T.astype(BF16)
        diag[...] = block_diag(proj_t)
        pieces = block[tile:].astype(F32)
        sender = pieces[0:3] + pieces[3:6] + pieces[6:9]
        receiver = col_pos[row_tile ^ me_col]
        square = jnp.zeros((tile, tile), F32)
        separation = []
        for k in range(3):
            up = jnp.broadcast_to(receiver[k : k + 1], (tile, tile)).T
            separation.append(up - sender[k : k + 1])
            square = square + separation[k] * separation[k]
        distance = jnp.sqrt(square + SOFTENING)
        angle = (math.pi / CUTOFF) * distance
        mask = masks[slot].astype(F32)
        sine, cosine = sin_cos(angle)
        cut = 0.5 * (cosine + 1.0) * mask
        dist[...] = fold(distance * SCALE)
        coef_h[...] = fold(-LN2 * cut)
        coef_x[...] = fold(sine / (cosine + 1.0) * (LN2 * math.pi / CUTOFF / TANGENT))
        inverse = 1.0 / distance
        for k in range(3):
            geom_out[slot, k] = fold(separation[k] * inverse)
        geom_out[slot, 3] = fold((-0.5 * math.pi / CUTOFF) * sine * mask)
        geom_out[slot, 4] = fold(cut * TANGENT)
        c_hi, c_lo = split2(cut)
        bias_part = (dot(c_hi, proj_t) + dot(c_lo, proj_t)) * b_f2[...]

        d, h, x = dist[...], coef_h[...], coef_x[...]
        for u in range(tile // 2):
            offset = d[u : u + 1] - centers
            gauss = jnp.exp2(-(offset * offset))
            gauss = gauss.astype(BF16)
            basis = jnp.concatenate([gauss, ones], axis=0)
            bend = jnp.tanh(dot(lhs[...], basis))
            value = lax.log2(1.0 - bend).astype(BF16)
            along = dot(lhs_t[...], offset.astype(BF16) * gauss).astype(BF16)
            slope = (1.0 + bend).astype(BF16) * along
            left[pl.ds(u * hidden, hidden), :] = spread(h[u : u + 1], hidden) * value
            tangents[slot, u] = spread(x[u : u + 1], hidden) * value + slope
        mixed = dot(left[...], diag[...])
        sums = [
            jnp.sum(mixed[u * hidden : (u + 1) * hidden] * w2[...], axis=0, keepdims=True)
            for u in range(tile // 2)
        ]
        rows[...] = jnp.concatenate(sums, axis=0)

        here = pl.ds(pl.multiple_of(row_tile * tile, tile), tile)
        msg[here, :] = msg[here, :] + (bias_part + unfold(rows[...]))

    msg16[...] = msg[...].astype(BF16)


def force_kernel(
    count, pairs, msg_a, msg_b, near, w_o1, b_o1, w_o2, b_o2, direction, w2_16, b_f2,
    proj, geom, tangents,
    features_hbm, keep, send, row_keep, row_send,
    features_out, grads, pre_act, diag, rows, left, force, row_force, sems,
):
    n_row = lax.axis_size("row")
    n_col = lax.axis_size("col")
    me_row = lax.axis_index("row")
    me_col = lax.axis_index("col")
    n_feat, tile = features_out.shape
    hidden = w2_16.shape[0]
    force[...] = jnp.zeros_like(force)
    row_force[...] = jnp.zeros_like(row_force)
    messages = (msg_a[...] + msg_b[...].astype(F32)).astype(BF16)
    pre = dot(messages, w_o1[...]) + b_o1[...]
    pre_act[...] = pre
    s_hi, s_lo = split2(direction[0:1] / (1.0 + jnp.exp(-pre)))
    grads[...] = dot_t(s_hi, w_o1[...]) + dot_t(s_lo, w_o1[...])
    own = pre_act[pl.ds(pl.multiple_of(me_col * tile, tile), tile), :]
    active = jnp.maximum(own, 0.0) + jnp.log(1.0 + jnp.exp(-jnp.abs(own))) - LN2
    update = dot(active.astype(BF16), w_o2[...]) + b_o2[...]
    features_out[...] = (near[0, :n_feat].astype(F32) + update.T).astype(BF16)
    store = pltpu.make_async_copy(features_out, features_hbm, sems.at[0])
    store.start()

    @pl.loop(0, count[0, 0])
    def _(slot):
        row_tile, col_tile = pairs[0, 0, 0, slot], pairs[0, 0, 1, slot]
        here = pl.ds(pl.multiple_of(row_tile * tile, tile), tile)
        grad_rows = grads[here, :]
        left_rows = fold(grad_rows)
        rows[...] = left_rows
        diag[...] = block_diag(proj[slot])

        g = rows[...]
        for u in range(tile // 2):
            left[pl.ds(u * hidden, hidden), :] = w2_16[...] * spread(g[u : u + 1], hidden)
        mixed = dot(left[...], diag[...])
        sums = [
            jnp.sum(
                mixed[u * hidden : (u + 1) * hidden] * tangents[slot, u].astype(F32),
                axis=0,
                keepdims=True,
            )
            for u in range(tile // 2)
        ]
        rows[...] = jnp.concatenate(sums, axis=0)

        g_hi, g_lo = split2(grad_rows * b_f2[...])
        bias_part = dot(g_hi, proj[slot]) + dot(g_lo, proj[slot])
        dist_grad = unfold(geom[slot, 4] * rows[...]) + unfold(geom[slot, 3]) * bias_part
        to_rows, to_cols = [], []
        for k in range(3):
            push = unfold(geom[slot, k]) * dist_grad
            to_cols.append(jnp.sum(push, axis=0, keepdims=True))
            to_rows.append(-jnp.sum(push.T, axis=0, keepdims=True))
        zero = jnp.zeros((1, tile), F32)
        place = reverse_bits(col_tile ^ me_row, n_row)
        force[place] = force[place] + jnp.concatenate(to_cols + [zero], axis=0)
        place = reverse_bits(row_tile ^ me_col, n_col)
        row_force[place] = row_force[place] + jnp.concatenate(to_rows + [zero], axis=0)

    keep[...] = force[: n_row // 2]
    send[...] = force[n_row // 2 :]
    row_keep[...] = row_force[: n_col // 2]
    row_send[...] = row_force[n_col // 2 :]
    store.wait()


def exchange(value, axis, size, step):
    return lax.ppermute(value, axis, [(i, i ^ step) for i in range(size)])


ANY = pl.BlockSpec(memory_space=pl.ANY)
SMEM = pl.BlockSpec(memory_space=pltpu.SMEM)
VMEM = pl.BlockSpec(memory_space=pltpu.VMEM)
HBM = pl.BlockSpec(memory_space=pltpu.HBM)


def run(kernel, name, specs, out_shape, scratch, limit, *operands):
    return pl.pallas_call(
        kernel,
        in_specs=specs,
        out_specs=[pl.BlockSpec(memory_space=x.memory_space) for x in out_shape],
        out_shape=out_shape,
        scratch_shapes=scratch,
        compiler_params=pltpu.CompilerParams(vmem_limit_bytes=limit * MIB),
        name=name,
    )(*operands)


def local(
    features, positions, tile_pairs, pair_count, masks,
    w_in, w_f1, b_f1, w_f2, b_f2, w_o1, b_o1, w_o2, b_o2, read_w,
):
    n_feat, owned = features.shape
    tile = masks.shape[-1]
    tp = masks.shape[2]
    n_row = lax.axis_size("row")
    n_col = lax.axis_size("col")
    span = n_col * owned
    half = tile // 2
    nbasis, hidden = w_f1.shape

    near, col_pos = run(
        pack_kernel, "pack_tile", [HBM, HBM],
        [out_type((1, n_feat + POS_ROWS, owned), BF16), out_type((1, 8, owned), F32)],
        [
            pltpu.VMEM(features.shape, BF16),
            pltpu.VMEM(positions.shape, F32),
            pltpu.SemaphoreType.DMA((2,)),
        ],
        60,
        features, positions,
    )
    lhs, lhs_t, w2, w2_16, w_in_t, direction, w_o2, w_o1, b_f2, b_o1, b_o2, masks, pairs = run(
        weight_kernel, "weight_tables", [HBM] * 12,
        [
            out_type((hidden, nbasis + 16), BF16),
            out_type((hidden, nbasis), BF16),
            out_type((hidden, 2 * n_feat), F32),
            out_type((hidden, 2 * n_feat), BF16),
            out_type((n_feat, n_feat), BF16),
            out_type((8, n_feat), F32),
            out_type(w_o2.shape, BF16),
            out_type(w_o1.shape, BF16),
        ]
        + [out_type((1, n_feat), F32)] * 3
        + [out_type((tp, tile, tile), jnp.int32), pltpu.SMEM(tile_pairs.shape, jnp.int32)],
        [
            pltpu.VMEM(w_in.shape, BF16),
            pltpu.VMEM(w_f1.shape, BF16),
            pltpu.VMEM((1, hidden), F32),
            pltpu.VMEM(w_f2.shape, BF16),
            pltpu.VMEM((1, n_feat), F32),
            pltpu.SemaphoreType.DMA((12,)),
        ],
        60,
        w_in, w_f1, b_f1[None], w_f2, read_w[None], w_o2, w_o1, b_f2[None], b_o1[None], b_o2[None],
        masks[0, 0], tile_pairs,
    )
    col_pos = col_pos
    step = 1
    while step < n_col:
        col_pos = jnp.concatenate([col_pos, exchange(col_pos, "col", n_col, step)], axis=0)
        step *= 2

    def stack(held, got, *after):
        return run(
            stack_kernel, "stack_tiles", [VMEM, VMEM] + [ANY] * len(after),
            [out_type((2 * held.shape[0],) + held.shape[1:], BF16)], [], 4,
            held, got, *after,
        )[0]

    ready = [[w2], [col_pos]]
    own = near
    for steps in zip(*stage_orders(n_row)):
        pairs_of_rows = [(i, i ^ steps[i % 2]) for i in range(n_row)]
        got = lax.ppermute(near, "row", pairs_of_rows)
        near = stack(near, got, *(ready.pop(0) if ready else []))
    far = exchange(near, "row", n_row, 1)
    count = pair_count

    plane = pltpu.VMEM((half, 2 * tile), F32)
    partial, partial16, tangents, proj, geom = run(
        pair_kernel, "pair_messages", [SMEM, SMEM] + [VMEM] * 9,
        [
            out_type((span, n_feat), F32),
            out_type((span, n_feat), BF16),
            out_type((tp, half, n_feat, 2 * tile), BF16),
            out_type((tp, n_feat, tile), BF16),
            out_type((tp, 5, half, 2 * tile), F32),
        ],
        [
            pltpu.VMEM((2 * tile, 2 * n_feat), BF16),
            plane, plane, plane, plane,
            pltpu.VMEM((half * hidden, 2 * tile), BF16),
        ],
        16,
        count, pairs, near, far, col_pos, masks, lhs, lhs_t, w2, w_in_t, b_f2,
    )

    step = 1
    while step < n_col // 2:
        partial = partial + exchange(partial16, "col", n_col, step).astype(F32)
        partial16 = partial.astype(BF16)
        step *= 2
    other = exchange(partial16, "col", n_col, step)

    features_out, keep, send, row_keep, row_send = run(
        force_kernel, "pair_forces",
        [SMEM, SMEM] + [VMEM] * 13,
        [
            pltpu.HBM((n_feat, owned), BF16),
            out_type((n_row // 2, 4, owned), F32),
            out_type((n_row // 2, 4, owned), F32),
            out_type((n_col // 2, 4, owned), F32),
            out_type((n_col // 2, 4, owned), F32),
        ],
        [
            pltpu.VMEM((n_feat, owned), BF16),
            pltpu.VMEM((span, n_feat), F32),
            pltpu.VMEM((span, n_feat), F32),
            pltpu.VMEM((2 * tile, 2 * n_feat), BF16),
            plane,
            pltpu.VMEM((half * hidden, 2 * n_feat), BF16),
            pltpu.VMEM((n_row, 4, owned), F32),
            pltpu.VMEM((n_col, 4, owned), F32),
            pltpu.SemaphoreType.DMA((1,)),
        ],
        16,
        count, pairs, partial, other, own, w_o1, b_o1, w_o2, b_o2, direction, w2_16, b_f2,
        proj, geom, tangents,
    )

    def reduce_halves(keep, send, axis, size):
        step = 1
        while True:
            other = exchange(send, axis, size, step)
            half = keep.shape[0] // 2
            step *= 2
            if step == size:
                return (keep + other)[0]
            send = keep[half:] + other[half:]
            keep = keep[:half] + other[:half]

    forces = reduce_halves(keep, send, "row", n_row) + reduce_halves(
        row_keep, row_send, "col", n_col
    )
    return (features_out, forces[:3])


def solution(mesh):
    atoms = P(None, ("row", "col"))
    in_specs = (
        atoms,
        atoms,
        P("row", "col", None, None),
        P("row", "col"),
        P("row", "col", None, None, None),
    ) + (P(),) * 10
    return jax.shard_map(
        local, mesh=mesh, in_specs=in_specs, out_specs=(atoms, atoms), check_vma=False
    )
```
